32 devices in a mesh: section: 4 (over y, x), tensor: 2 (over core), dp: 4 (over z).
Axes of the slice: x: 2, y: 2, z: 4, core: 2. Of those that a mesh axis runs over, the one named last changes fastest.
Arguments:
- fwd_input: bfloat16 [4, 4, 128, 8192], P('dp', 'section', None, 'tensor'), may hold values from -6 to 6
- fwd_positions: int32 [4, 4, 128], P('dp', 'section'), may hold values from 0 to 4095
- key_weight: bfloat16 [4, 8192, 4, 128], P('section', 'tensor'), may hold values from -0.0625 to 0.0625
- stash: bfloat16 [4, 4, 128, 8192], P('dp', 'section', None, 'tensor'), may hold values from -0.26367188 to 0.26367188
- partner: int32 [4], replicated, may hold values from 0 to 3, as said below
- key_grad: bfloat16 [4, 4, 128, 4, 128], P('dp', 'section'), may hold values from -6 to 6
- bwd_positions: int32 [4, 4, 128], P('dp', 'section'), may hold values from 0 to 4095
Outputs:
- key_out: bfloat16 [4, 4, 128, 4, 128], P('dp', 'section', 'tensor')
- grad_in: bfloat16 [4, 4, 128, 8192], P('dp', 'section', None, 'tensor')
- evicted: bfloat16 [4, 4, 128, 8192], P('dp', 'section', None, 'tensor')
- weight_grad: bfloat16 [4, 8192, 4, 128], P('section', ('tensor', 'dp'))
The draws below stay inside these ranges and needn't reach their ends.
Inputs may be any that keep to these rules, and one draw needn't show every extreme that they name: partner[s] = s xor k for one k with 2 <= k < 4, the same k for all sections; it pairs every section of the first half with one of the second half.
All inputs are finite; a program needn't handle non-finite values.
Results may differ from the reference program's by a relative error of at most 0.015.
Values may be sent and summed in bfloat16 or wider, within the bound.
No kernel may reach another device: no remote copies, remote signals or barrier semaphores. Data moves between devices by JAX's collectives and lax.ppermute only.
A program may use at most 64 MiB of HBM per device.

```python
import jax
import jax.numpy as jnp
from jax import lax

D = 8192
KVH = 4
HD = 128
ROWS = 128
SEQ = 4096
N_SECTION = 4
N_DP = 4


def draw_partner(key, part):
    mask_value = jax.random.randint(key, (), N_SECTION // 2, N_SECTION, dtype=jnp.int32)
    return jnp.bitwise_xor(jnp.arange(N_SECTION, dtype=jnp.int32), mask_value)


def set_ends(entries, own_key, smallest, top_value):
    longest = entries.shape.index(max(entries.shape))
    spots = []
    for shift in (0, 1):
        where = [jax.random.randint(jax.random.fold_in(own_key, axis), (), 0, length) for axis, length in enumerate(entries.shape)]
        where[longest] = (where[longest] + shift) % entries.shape[longest]
        spots.append(tuple(where))
    return entries.at[spots[0]].set(smallest).at[spots[1]].set(top_value)


def block_scale(rng, dims, pieces, least, high):
    factor_of, own = 1.0, jax.random.fold_in(rng, 6)
    for dim, blocks in pieces:
        steps = jnp.exp(jax.random.uniform(jax.random.fold_in(own, dim), (blocks,), jnp.float32, least / len(pieces), high / len(pieces)))
        factor_of = factor_of * jnp.repeat(steps, dims[dim] // blocks).reshape([-1 if axis == dim else 1 for axis in range(len(dims))])
    return factor_of


def gaussian(stream_key, extent, spread, reach, cuts=(), kind=jnp.bfloat16):
    result = jax.random.normal(stream_key, extent, jnp.float32) * spread
    if len(cuts) > 0:
        result = block_scale(stream_key, extent, cuts, -0.22, 0.18) * result
    return jnp.clip(result, min=-reach, max=reach).astype(kind)


def setup_inputs(seed: int = 0) -> dict:
    key_list = jax.random.split(jax.random.key(seed), 8)
    fwd_input = gaussian(key_list[0], (N_DP, N_SECTION, ROWS, D), 1.0, 6.0, ((0, 4), (1, 4), (3, 2)))
    fwd_positions = set_ends(jax.random.randint(key_list[1], (N_DP, N_SECTION, ROWS), 0, SEQ), jax.random.fold_in(key_list[1], 1), 0, SEQ - 1).astype(jnp.int32)
    key_weight = gaussian(key_list[2], (N_SECTION, D, KVH, HD), D ** -0.5, 0.0625, ((0, 4), (1, 2)))
    stash = gaussian(key_list[3], (N_DP, N_SECTION, ROWS, D), ((ROWS * N_DP) ** -0.5), 0.26367188, ((0, 4), (1, 4), (3, 2)))
    partner = draw_partner(jax.random.fold_in(key_list[7], 71), 0)
    key_grad = gaussian(key_list[5], (N_DP, N_SECTION, ROWS, KVH, HD), 1.0, 6.0, ((0, 4), (1, 4)))
    bwd_positions = set_ends(jax.random.randint(key_list[6], (N_DP, N_SECTION, ROWS), 0, SEQ), jax.random.fold_in(key_list[6], 1), 0, SEQ - 1).astype(jnp.int32)
    return dict(fwd_input=fwd_input, fwd_positions=fwd_positions, key_weight=key_weight, stash=stash, partner=partner, key_grad=key_grad, bwd_positions=bwd_positions)


THETA = 500000.0


def rope_tables(positions, head_size):
    half = head_size // 2
    freqs = THETA ** (-(2.0 * jnp.arange(half, dtype=jnp.float32)) / head_size)
    angles = positions.astype(jnp.float32)[..., None] * freqs
    return jnp.cos(angles), jnp.sin(angles)


def rotate(keys, cosine, sine, sign):
    half = keys.shape[-1] // 2
    first = keys[..., :half]
    second = keys[..., half:]
    return jnp.concatenate([first * cosine - sign * second * sine, second * cosine + sign * first * sine], axis=-1)


def section_work(section, fwd_input, fwd_positions, key_weight, stash, partner, key_grad, bwd_positions):
    inputs = fwd_input[:, section].astype(jnp.float32)
    weight = key_weight[section].astype(jnp.float32)
    proj = jnp.einsum('prd,dhe->prhe', inputs, weight)
    cosine, sine = rope_tables(fwd_positions[:, section], HD)
    key_block = rotate(proj, cosine[:, :, None], sine[:, :, None], 1.0).astype(jnp.bfloat16)
    grads = key_grad[:, section].astype(jnp.float32)
    back_cos, back_sin = rope_tables(bwd_positions[:, section], HD)
    grad_pre = rotate(grads, back_cos[:, :, None], back_sin[:, :, None], -1.0).astype(jnp.bfloat16)
    grad_wide = grad_pre.astype(jnp.float32)
    input_grad = jnp.einsum('prhe,dhe->prd', grad_wide, weight).astype(jnp.bfloat16)
    held = stash[:, partner[section]].astype(jnp.float32)
    parts = jnp.einsum('prd,prhe->pdhe', held, grad_wide).astype(jnp.bfloat16)
    parts = lax.optimization_barrier(parts).astype(jnp.float32)
    weight_grad = jnp.sum(parts, axis=0).astype(jnp.bfloat16)
    return key_block, input_grad, weight_grad


def reference(fwd_input, fwd_positions, key_weight, stash, partner, key_grad, bwd_positions):
    def one_section(section):
        return section_work(section, fwd_input, fwd_positions, key_weight, stash, partner, key_grad, bwd_positions)

    key_all, input_all, weight_grad = lax.map(one_section, jnp.arange(N_SECTION, dtype=jnp.int32))
    key_out = jnp.moveaxis(key_all, 0, 1)
    grad_in = jnp.roll(jnp.moveaxis(input_all, 0, 1), -1, axis=1)
    evicted = jnp.take(fwd_input, partner, axis=1)
    return key_out, grad_in, evicted, weight_grad
```

```python
import jax
import jax.numpy as jnp
from jax import lax
from jax.sharding import PartitionSpec as P

THETA = 500000.0


def shifted(value, axis, distance):
    size = lax.axis_size(axis)
    return lax.ppermute(value, axis, [(i, (i + distance) % size) for i in range(size)])


def swapped(value, axis, mask):
    size = lax.axis_size(axis)
    return lax.ppermute(value, axis, [(i, i ^ mask) for i in range(size)])


def after(value, earlier):
    return lax.optimization_barrier((value, earlier))[0]


def rope_tables(positions, head_size):
    half = head_size // 2
    freqs = THETA ** (-(2.0 * jnp.arange(half, dtype=jnp.float32)) / head_size)
    angles = positions.astype(jnp.float32)[..., None] * freqs
    return (jnp.cos(angles), jnp.sin(angles))


def rotate(keys, cosine, sine, sign):
    half = keys.shape[-1] // 2
    first = keys[..., :half]
    second = keys[..., half:]
    return jnp.concatenate(
        [first * cosine - sign * second * sine, second * cosine + sign * first * sine], axis=-1
    )


def work(mask, inputs, fwd_positions, weight, stash, key_grad, bwd_positions):
    width, heads, head_size = weight.shape
    rows = inputs.shape[0]
    flat_weight = weight.reshape(width, heads * head_size)

    held = swapped(stash, "section", mask)
    evicted = swapped(after(inputs, held), "section", mask)

    back_cos, back_sin = rope_tables(bwd_positions, head_size)
    grad_pre = rotate(
        key_grad.astype(jnp.float32), back_cos[:, None], back_sin[:, None], -1.0
    ).astype(jnp.bfloat16)
    grad_flat = grad_pre.reshape(rows, heads * head_size)
    replicas = lax.axis_size("dp")
    grads_all = [grad_flat] + [shifted(grad_flat, "dp", j) for j in range(1, replicas)]

    input_grad = jnp.einsum(
        "rn,dn->rd", grad_flat, flat_weight, preferred_element_type=jnp.float32
    ).astype(jnp.bfloat16)
    grad_in = shifted(after(input_grad, evicted), "section", -1)

    products = jnp.dot(inputs, flat_weight, preferred_element_type=jnp.float32)
    members = lax.axis_size("tensor")
    me = lax.axis_index("tensor")
    my_rows = rows // members
    summed = lax.dynamic_slice_in_dim(products, me * my_rows, my_rows, 0)
    for j in range(1, members):
        other = lax.dynamic_slice_in_dim(products, (me + j) % members * my_rows, my_rows, 0)
        summed = summed + shifted(other.astype(jnp.bfloat16), "tensor", j).astype(jnp.float32)
    my_positions = lax.dynamic_slice_in_dim(fwd_positions, me * my_rows, my_rows, 0)
    cosine, sine = rope_tables(my_positions, head_size)
    key_out = rotate(
        summed.reshape(my_rows, heads, head_size), cosine[:, None], sine[:, None], 1.0
    ).astype(jnp.bfloat16)

    share = width // replicas
    replica = lax.axis_index("dp")
    rows_all = []
    for j in range(replicas):
        block = lax.dynamic_slice_in_dim(held, (replica + j) % replicas * share, share, 1)
        rows_all.append(shifted(block, "dp", j) if j else block)
    weight_grad = lax.dot_general(
        jnp.concatenate(rows_all, 0),
        jnp.concatenate(grads_all, 0),
        (((0,), (0,)), ((), ())),
        preferred_element_type=jnp.float32,
    ).astype(jnp.bfloat16)
    return key_out, grad_in, evicted, weight_grad.reshape(share, heads, head_size)


def body(fwd_input, fwd_positions, key_weight, stash, partner, key_grad, bwd_positions):
    sections = lax.axis_size("section")
    first = sections // 2
    branches = [
        lambda *blocks, mask=mask: work(mask, *blocks) for mask in range(first, sections)
    ]
    key_out, grad_in, evicted, weight_grad = lax.switch(
        partner[0] - first,
        branches,
        fwd_input[0, 0],
        fwd_positions[0, 0],
        key_weight[0],
        stash[0, 0],
        key_grad[0, 0],
        bwd_positions[0, 0],
    )
    return key_out[None, None], grad_in[None, None], evicted[None, None], weight_grad[None]


def solution(mesh):
    placed = (
        P("dp", "section", None, "tensor"),
        P("dp", "section", None),
        P("section", "tensor", None, None),
        P("dp", "section", None, "tensor"),
        P(),
        P("dp", "section", None, None, None),
        P("dp", "section", None),
    )
    return jax.shard_map(
        body,
        mesh=mesh,
        in_specs=placed,
        out_specs=(
            P("dp", "section", "tensor", None, None),
            P("dp", "section", None, "tensor"),
            P("dp", "section", None, "tensor"),
            P("section", ("tensor", "dp"), None, None),
        ),
        check_vma=False,
    )
```

```python
import math

import jax
import jax.numpy as jnp
from jax import lax
from jax.experimental import pallas as pl
from jax.experimental.layout import Layout, with_layout_constraint
from jax.experimental.pallas import tpu as pltpu
from jax.sharding import PartitionSpec as P

THETA = 500000.0


def shifted(value, axis, distance):
    size = lax.axis_size(axis)
    return lax.ppermute(value, axis, [(i, (i + distance) % size) for i in range(size)])


def swapped(value, axis, mask):
    size = lax.axis_size(axis)
    return lax.ppermute(value, axis, [(i, i ^ mask) for i in range(size)])


def row_major(value):
    return with_layout_constraint(value, Layout(major_to_minor=tuple(range(value.ndim))))


def exchanged(blocks):
    got = lax.all_to_all(row_major(blocks), "dp", split_axis=0, concat_axis=0, tiled=True)
    return row_major(got)


def after(value, earlier):
    return lax.optimization_barrier((value, earlier))[0]


def rope_tables(positions, head_size):
    half = head_size // 2
    freqs = THETA ** (-(2.0 * jnp.arange(half, dtype=jnp.float32)) / head_size)
    angles = positions.astype(jnp.float32)[..., None] * freqs
    return (jnp.cos(angles), jnp.sin(angles))


def rotate(keys, cosine, sine, sign):
    half = keys.shape[-1] // 2
    first = keys[..., :half]
    second = keys[..., half:]
    return jnp.concatenate(
        [first * cosine - sign * second * sine, second * cosine + sign * first * sine], axis=-1
    )


def store_kernel(*refs):
    count = len(refs) - 2
    parts, out, sems = refs[:count], refs[count], refs[count + 1]
    rows = out.shape[0] // count
    copies = [
        pltpu.make_async_copy(part, out.at[pl.ds(i * rows, rows)], sems.at[i])
        for i, part in enumerate(parts)
    ]
    for copy in copies:
        copy.start()
    for copy in copies:
        copy.wait()


def stored(*parts):
    shape = (sum(part.shape[0] for part in parts),) + parts[0].shape[1:]
    size = 2 * parts[0].dtype.itemsize * math.prod(shape)
    return pl.pallas_call(
        store_kernel,
        out_shape=pltpu.HBM(shape, parts[0].dtype),
        in_specs=[pl.BlockSpec(memory_space=pl.ANY)] * len(parts),
        out_specs=pl.BlockSpec(memory_space=pl.ANY),
        scratch_shapes=[pltpu.SemaphoreType.DMA((len(parts),))],
        cost_estimate=pl.CostEstimate(flops=0, bytes_accessed=size, transcendentals=0),
    )(*[pltpu.with_memory_space_constraint(part, pltpu.VMEM) for part in parts])


def work(mask, inputs, fwd_positions, weight, stash, key_grad, bwd_positions):
    width, heads, head_size = weight.shape
    rows = inputs.shape[0]
    flat_weight = weight.reshape(width, heads * head_size)

    evicted = swapped(inputs, "section", mask)

    replicas = lax.axis_size("dp")
    share = width // replicas
    split = jnp.stack([stash[:, i * share : (i + 1) * share] for i in range(replicas)])
    blocks = exchanged(split).reshape(replicas * rows, share)
    half = replicas * rows // 2
    held = [swapped(blocks[i * half : (i + 1) * half], "section", mask) for i in range(2)]

    back_cos, back_sin = rope_tables(bwd_positions, head_size)
    grad_pre = rotate(
        key_grad.astype(jnp.float32), back_cos[:, None], back_sin[:, None], -1.0
    ).astype(jnp.bfloat16)
    grad_flat = grad_pre.reshape(rows, heads * head_size)
    grads_all = exchanged(jnp.broadcast_to(grad_flat, (replicas, *grad_flat.shape)))

    input_grad = jnp.einsum(
        "rn,dn->rd", grad_flat, flat_weight, preferred_element_type=jnp.float32
    ).astype(jnp.bfloat16)
    grad_in = shifted(after(input_grad, blocks), "section", -1)

    products = jnp.dot(inputs, flat_weight, preferred_element_type=jnp.float32)
    members = lax.axis_size("tensor")
    me = lax.axis_index("tensor")
    my_rows = rows // members
    summed = lax.dynamic_slice_in_dim(products, me * my_rows, my_rows, 0)
    for j in range(1, members):
        other = lax.dynamic_slice_in_dim(products, (me + j) % members * my_rows, my_rows, 0)
        summed = summed + shifted(other.astype(jnp.bfloat16), "tensor", j).astype(jnp.float32)
    my_positions = lax.dynamic_slice_in_dim(fwd_positions, me * my_rows, my_rows, 0)
    cosine, sine = rope_tables(my_positions, head_size)
    key_out = rotate(
        summed.reshape(my_rows, heads, head_size), cosine[:, None], sine[:, None], 1.0
    ).astype(jnp.bfloat16)

    weight_grad = lax.dot_general(
        jnp.concatenate(held, 0),
        grads_all.reshape(replicas * rows, heads * head_size),
        (((0,), (0,)), ((), ())),
        preferred_element_type=jnp.float32,
    ).astype(jnp.bfloat16)
    weight_grad = weight_grad.reshape(share, heads, head_size)
    return stored(key_out), stored(grad_in), stored(evicted), stored(weight_grad)


def body(fwd_input, fwd_positions, key_weight, stash, partner, key_grad, bwd_positions):
    sections = lax.axis_size("section")
    first = sections // 2
    branches = [
        lambda *blocks, mask=mask: work(mask, *blocks) for mask in range(first, sections)
    ]
    key_out, grad_in, evicted, weight_grad = lax.switch(
        partner[0] - first,
        branches,
        fwd_input[0, 0],
        fwd_positions[0, 0],
        key_weight[0],
        stash[0, 0],
        key_grad[0, 0],
        bwd_positions[0, 0],
    )
    return key_out[None, None], grad_in[None, None], evicted[None, None], weight_grad[None]


def solution(mesh):
    placed = (
        P("dp", "section", None, "tensor"),
        P("dp", "section", None),
        P("section", "tensor", None, None),
        P("dp", "section", None, "tensor"),
        P(),
        P("dp", "section", None, None, None),
        P("dp", "section", None),
    )
    return jax.shard_map(
        body,
        mesh=mesh,
        in_specs=placed,
        out_specs=(
            P("dp", "section", "tensor", None, None),
            P("dp", "section", None, "tensor"),
            P("dp", "section", None, "tensor"),
            P("section", ("tensor", "dp"), None, None),
        ),
        check_vma=False,
    )
```

```python
import functools

import jax
import jax.numpy as jnp
from jax import lax
from jax.experimental import pallas as pl
from jax.experimental.pallas import tpu as pltpu
from jax.sharding import PartitionSpec as P

THETA = 500000.0


def shifted(value, axis, distance):
    size = lax.axis_size(axis)
    return lax.ppermute(value, axis, [(i, (i + distance) % size) for i in range(size)])


def swapped(value, axis, mask):
    size = lax.axis_size(axis)
    return lax.ppermute(value, axis, [(i, i ^ mask) for i in range(size)])


def after(value, earlier):
    return lax.optimization_barrier((value, earlier))[0]


def rope_tables(positions, head_size):
    half = head_size // 2
    freqs = THETA ** (-(2.0 * jnp.arange(half, dtype=jnp.float32)) / head_size)
    angles = positions.astype(jnp.float32)[..., None] * freqs
    return (jnp.cos(angles), jnp.sin(angles))


def rotate(keys, cosine, sine, sign):
    half = keys.shape[-1] // 2
    first = keys[..., :half]
    second = keys[..., half:]
    return jnp.concatenate(
        [first * cosine - sign * second * sine, second * cosine + sign * first * sine], axis=-1
    )


def store_kernel(start, *refs):
    part, out, sem = refs[0], refs[-2], refs[-1]
    copy = pltpu.make_async_copy(part, out.at[pl.ds(start, part.shape[0])], sem)
    copy.start()
    copy.wait()


def stored(part, total=None, start=0, into=None):
    shape = (total or part.shape[0],) + part.shape[1:]
    operands = [pltpu.with_memory_space_constraint(part, pltpu.VMEM)]
    if into is not None:
        operands.append(pltpu.with_memory_space_constraint(into, pltpu.HBM))
    return pl.pallas_call(
        functools.partial(store_kernel, start),
        out_shape=pltpu.HBM(shape, part.dtype),
        in_specs=[pl.BlockSpec(memory_space=pl.ANY)] * len(operands),
        out_specs=pl.BlockSpec(memory_space=pl.ANY),
        scratch_shapes=[pltpu.SemaphoreType.DMA],
        input_output_aliases={} if into is None else {1: 0},
        cost_estimate=pl.CostEstimate(
            flops=0, bytes_accessed=2 * part.size * part.dtype.itemsize, transcendentals=0
        ),
    )(*operands)


def work(mask, inputs, fwd_positions, weight, stash, key_grad, bwd_positions):
    width, heads, head_size = weight.shape
    rows = inputs.shape[0]

    held = swapped(stash, "section", mask)
    evicted = swapped(inputs, "section", mask)

    replicas = lax.axis_size("dp")
    replica = lax.axis_index("dp")
    share = width // replicas
    blocks = [
        lax.dynamic_slice_in_dim(held, (replica + j) % replicas * share, share, 1)
        for j in range(replicas)
    ]
    rows_all = [shifted(block, "dp", j) if j else block for j, block in enumerate(blocks)]
    flat_weight = after(weight, blocks).reshape(width, heads * head_size)

    back_cos, back_sin = rope_tables(bwd_positions, head_size)
    grad_pre = rotate(
        key_grad.astype(jnp.float32), back_cos[:, None], back_sin[:, None], -1.0
    ).astype(jnp.bfloat16)
    grad_flat = grad_pre.reshape(rows, heads * head_size)
    grads_all = lax.all_to_all(
        jnp.broadcast_to(grad_flat, (replicas, *grad_flat.shape)), "dp", 0, 0, tiled=True
    )
    grads_all = [
        lax.dynamic_index_in_dim(grads_all, (replica - j) % replicas, 0, keepdims=False)
        for j in range(replicas)
    ]

    input_grad = jnp.einsum(
        "rn,dn->rd", grad_flat, flat_weight, preferred_element_type=jnp.float32
    ).astype(jnp.bfloat16)
    grad_in = shifted(input_grad, "section", -1)

    products = jnp.dot(inputs, flat_weight, preferred_element_type=jnp.float32)
    members = lax.axis_size("tensor")
    me = lax.axis_index("tensor")
    my_rows = rows // members
    summed = lax.dynamic_slice_in_dim(products, me * my_rows, my_rows, 0)
    for j in range(1, members):
        other = lax.dynamic_slice_in_dim(products, (me + j) % members * my_rows, my_rows, 0)
        summed = summed + shifted(other.astype(jnp.bfloat16), "tensor", j).astype(jnp.float32)
    my_positions = lax.dynamic_slice_in_dim(fwd_positions, me * my_rows, my_rows, 0)
    cosine, sine = rope_tables(my_positions, head_size)
    key_out = rotate(
        summed.reshape(my_rows, heads, head_size), cosine[:, None], sine[:, None], 1.0
    ).astype(jnp.bfloat16)

    weight_grad = lax.dot_general(
        jnp.concatenate(rows_all, 0),
        jnp.concatenate(grads_all, 0),
        (((0,), (0,)), ((), ())),
        preferred_element_type=jnp.float32,
    ).astype(jnp.bfloat16)
    weight_grad = weight_grad.reshape(share, heads, head_size)

    return stored(key_out), stored(grad_in), stored(after(evicted, weight_grad)), stored(weight_grad)


def body(fwd_input, fwd_positions, key_weight, stash, partner, key_grad, bwd_positions):
    sections = lax.axis_size("section")
    first = sections // 2
    branches = [
        lambda *blocks, mask=mask: work(mask, *blocks) for mask in range(first, sections)
    ]
    key_out, grad_in, evicted, weight_grad = lax.switch(
        partner[0] - first,
        branches,
        fwd_input[0, 0],
        fwd_positions[0, 0],
        key_weight[0],
        stash[0, 0],
        key_grad[0, 0],
        bwd_positions[0, 0],
    )
    return key_out[None, None], grad_in[None, None], evicted[None, None], weight_grad[None]


def solution(mesh):
    placed = (
        P("dp", "section", None, "tensor"),
        P("dp", "section", None),
        P("section", "tensor", None, None),
        P("dp", "section", None, "tensor"),
        P(),
        P("dp", "section", None, None, None),
        P("dp", "section", None),
    )
    return jax.shard_map(
        body,
        mesh=mesh,
        in_specs=placed,
        out_specs=(
            P("dp", "section", "tensor", None, None),
            P("dp", "section", None, "tensor"),
            P("dp", "section", None, "tensor"),
            P("section", ("tensor", "dp"), None, None),
        ),
        check_vma=False,
    )
```

```python
import functools

import jax
import jax.numpy as jnp
from jax import lax
from jax.experimental import pallas as pl
from jax.experimental.pallas import tpu as pltpu
from jax.sharding import PartitionSpec as P

THETA = 500000.0


def shifted(value, axis, distance):
    size = lax.axis_size(axis)
    return lax.ppermute(value, axis, [(i, (i + distance) % size) for i in range(size)])


def swapped(value, axis, mask):
    size = lax.axis_size(axis)
    return lax.ppermute(value, axis, [(i, i ^ mask) for i in range(size)])


def after(value, earlier):
    return lax.optimization_barrier((value, earlier))[0]


def rope_tables(positions, head_size):
    half = head_size // 2
    freqs = THETA ** (-(2.0 * jnp.arange(half, dtype=jnp.float32)) / head_size)
    angles = positions.astype(jnp.float32)[..., None] * freqs
    return (jnp.cos(angles), jnp.sin(angles))


def rotate(keys, cosine, sine, sign):
    half = keys.shape[-1] // 2
    first = keys[..., :half]
    second = keys[..., half:]
    return jnp.concatenate(
        [first * cosine - sign * second * sine, second * cosine + sign * first * sine], axis=-1
    )


def store_kernel(start, *refs):
    part, out, sem = refs[0], refs[-2], refs[-1]
    copy = pltpu.make_async_copy(part, out.at[pl.ds(start, part.shape[0])], sem)
    copy.start()
    copy.wait()


def stored(part, total=None, start=0, into=None):
    shape = (total or part.shape[0],) + part.shape[1:]
    operands = [pltpu.with_memory_space_constraint(part, pltpu.VMEM)]
    if into is not None:
        operands.append(pltpu.with_memory_space_constraint(into, pltpu.HBM))
    return pl.pallas_call(
        functools.partial(store_kernel, start),
        out_shape=pltpu.HBM(shape, part.dtype),
        in_specs=[pl.BlockSpec(memory_space=pl.ANY)] * len(operands),
        out_specs=pl.BlockSpec(memory_space=pl.ANY),
        scratch_shapes=[pltpu.SemaphoreType.DMA],
        input_output_aliases={} if into is None else {1: 0},
        cost_estimate=pl.CostEstimate(
            flops=0, bytes_accessed=2 * part.size * part.dtype.itemsize, transcendentals=0
        ),
    )(*operands)


def work(mask, inputs, fwd_positions, weight, stash, key_grad, bwd_positions):
    width, heads, head_size = weight.shape
    rows = inputs.shape[0]

    held = swapped(stash, "section", mask)
    evicted = swapped(inputs, "section", mask)

    replicas = lax.axis_size("dp")
    replica = lax.axis_index("dp")
    share = width // replicas
    blocks = [
        lax.dynamic_slice_in_dim(held, (replica + j) % replicas * share, share, 1)
        for j in range(replicas)
    ]
    rows_all = [shifted(block, "dp", j) if j else block for j, block in enumerate(blocks)]
    flat_weight = weight.reshape(width, heads * head_size)

    back_cos, back_sin = rope_tables(bwd_positions, head_size)
    grad_pre = rotate(
        key_grad.astype(jnp.float32), back_cos[:, None], back_sin[:, None], -1.0
    ).astype(jnp.bfloat16)
    grad_flat = grad_pre.reshape(rows, heads * head_size)
    grads_all = lax.all_to_all(
        jnp.broadcast_to(grad_flat, (replicas, *grad_flat.shape)), "dp", 0, 0, tiled=True
    )
    grads_all = [
        lax.dynamic_index_in_dim(grads_all, (replica - j) % replicas, 0, keepdims=False)
        for j in range(replicas)
    ]

    input_grad = jnp.einsum(
        "rn,dn->rd", grad_flat, flat_weight, preferred_element_type=jnp.float32
    ).astype(jnp.bfloat16)
    grad_in = shifted(after(input_grad, blocks), "section", -1)

    products = jnp.dot(after(inputs, rows_all[1:2]), flat_weight, preferred_element_type=jnp.float32)
    members = lax.axis_size("tensor")
    me = lax.axis_index("tensor")
    my_rows = rows // members
    summed = lax.dynamic_slice_in_dim(products, me * my_rows, my_rows, 0)
    for j in range(1, members):
        other = lax.dynamic_slice_in_dim(products, (me + j) % members * my_rows, my_rows, 0)
        summed = summed + shifted(other.astype(jnp.bfloat16), "tensor", j).astype(jnp.float32)
    my_positions = lax.dynamic_slice_in_dim(fwd_positions, me * my_rows, my_rows, 0)
    cosine, sine = rope_tables(my_positions, head_size)
    key_out = rotate(
        summed.reshape(my_rows, heads, head_size), cosine[:, None], sine[:, None], 1.0
    ).astype(jnp.bfloat16)

    weight_grad = lax.dot_general(
        jnp.concatenate(rows_all, 0),
        jnp.concatenate(grads_all, 0),
        (((0,), (0,)), ((), ())),
        preferred_element_type=jnp.float32,
    ).astype(jnp.bfloat16)
    weight_grad = weight_grad.reshape(share, heads, head_size)

    return stored(key_out), stored(grad_in), stored(after(evicted, weight_grad)), stored(weight_grad)


def body(fwd_input, fwd_positions, key_weight, stash, partner, key_grad, bwd_positions):
    sections = lax.axis_size("section")
    first = sections // 2
    branches = [
        lambda *blocks, mask=mask: work(mask, *blocks) for mask in range(first, sections)
    ]
    key_out, grad_in, evicted, weight_grad = lax.switch(
        partner[0] - first,
        branches,
        fwd_input[0, 0],
        fwd_positions[0, 0],
        key_weight[0],
        stash[0, 0],
        key_grad[0, 0],
        bwd_positions[0, 0],
    )
    return key_out[None, None], grad_in[None, None], evicted[None, None], weight_grad[None]


def solution(mesh):
    placed = (
        P("dp", "section", None, "tensor"),
        P("dp", "section", None),
        P("section", "tensor", None, None),
        P("dp", "section", None, "tensor"),
        P(),
        P("dp", "section", None, None, None),
        P("dp", "section", None),
    )
    return jax.shard_map(
        body,
        mesh=mesh,
        in_specs=placed,
        out_specs=(
            P("dp", "section", "tensor", None, None),
            P("dp", "section", None, "tensor"),
            P("dp", "section", None, "tensor"),
            P("section", ("tensor", "dp"), None, None),
        ),
        check_vma=False,
    )
```

```python
import functools

import jax
import jax.numpy as jnp
from jax import lax
from jax.experimental import pallas as pl
from jax.experimental.pallas import tpu as pltpu
from jax.sharding import PartitionSpec as P

THETA = 500000.0


def shifted(value, axis, distance):
    size = lax.axis_size(axis)
    return lax.ppermute(value, axis, [(i, (i + distance) % size) for i in range(size)])


def swapped(value, axis, mask):
    size = lax.axis_size(axis)
    return lax.ppermute(value, axis, [(i, i ^ mask) for i in range(size)])


def after(value, earlier):
    return lax.optimization_barrier((value, earlier))[0]


def rope_tables(positions, head_size):
    half = head_size // 2
    freqs = THETA ** (-(2.0 * jnp.arange(half, dtype=jnp.float32)) / head_size)
    angles = positions.astype(jnp.float32)[..., None] * freqs
    return (jnp.cos(angles), jnp.sin(angles))


def rotate(keys, cosine, sine, sign):
    half = keys.shape[-1] // 2
    first = keys[..., :half]
    second = keys[..., half:]
    return jnp.concatenate(
        [first * cosine - sign * second * sine, second * cosine + sign * first * sine], axis=-1
    )


def store_kernel(start, *refs):
    part, out, sems = refs[0], refs[-2], refs[-1]
    pieces = sems.shape[0]
    step = part.shape[0] // pieces
    copies = [
        pltpu.make_async_copy(
            part.at[pl.ds(i * step, step)], out.at[pl.ds(start + i * step, step)], sems.at[i]
        )
        for i in range(pieces)
    ]
    for copy in copies:
        copy.start()
    for copy in copies:
        copy.wait()


def stored(part, total=None, start=0, into=None):
    shape = (total or part.shape[0],) + part.shape[1:]
    pieces = 4 if part.shape[0] % 64 == 0 else 1
    operands = [pltpu.with_memory_space_constraint(part, pltpu.VMEM)]
    if into is not None:
        operands.append(pltpu.with_memory_space_constraint(into, pltpu.HBM))
    return pl.pallas_call(
        functools.partial(store_kernel, start),
        out_shape=pltpu.HBM(shape, part.dtype),
        in_specs=[pl.BlockSpec(memory_space=pl.ANY)] * len(operands),
        out_specs=pl.BlockSpec(memory_space=pl.ANY),
        scratch_shapes=[pltpu.SemaphoreType.DMA((pieces,))],
        input_output_aliases={} if into is None else {1: 0},
        cost_estimate=pl.CostEstimate(
            flops=0, bytes_accessed=2 * part.size * part.dtype.itemsize, transcendentals=0
        ),
    )(*operands)


def work(mask, inputs, fwd_positions, weight, stash, key_grad, bwd_positions):
    width, heads, head_size = weight.shape
    rows = inputs.shape[0]

    around = lax.axis_size("section") == 4 and mask == 2
    cut = rows // 4 if around else rows
    held = [swapped(stash[:cut], "section", mask)]
    if around:
        held.append(swapped(stash[cut:], "section", mask))

    replicas = lax.axis_size("dp")
    replica = lax.axis_index("dp")
    share = width // replicas
    blocks = [
        jnp.concatenate(
            [
                lax.dynamic_slice_in_dim(piece, (replica + j) % replicas * share, share, 1)
                for piece in held
            ]
        )
        for j in range(replicas)
    ]
    rows_all = [shifted(block, "dp", j) if j else block for j, block in enumerate(blocks)]
    flat_weight = weight.reshape(width, heads * head_size)

    back_cos, back_sin = rope_tables(bwd_positions, head_size)
    grad_pre = rotate(
        key_grad.astype(jnp.float32), back_cos[:, None], back_sin[:, None], -1.0
    ).astype(jnp.bfloat16)
    grad_flat = grad_pre.reshape(rows, heads * head_size)
    grads_all = lax.all_to_all(
        jnp.broadcast_to(grad_flat, (replicas, *grad_flat.shape)), "dp", 0, 0, tiled=True
    )
    grads_all = [
        lax.dynamic_index_in_dim(grads_all, (replica - j) % replicas, 0, keepdims=False)
        for j in range(replicas)
    ]

    input_grad = jnp.einsum(
        "rn,dn->rd", grad_flat, flat_weight, preferred_element_type=jnp.float32
    ).astype(jnp.bfloat16)
    if around:
        cut = rows // 2
        lower, ahead = after((input_grad[cut:], inputs), held[0])
        turned = lax.ppermute(lower, "section", [(0, 2), (2, 0)])
        evicted = swapped(ahead, "section", mask)
        odd = lax.axis_index("section") % 2 == 1
        lower = swapped(jnp.where(odd, lower, after(turned, blocks)), "section", 1)
        upper = shifted(after(input_grad[:cut], blocks), "section", -1)
        grad_in = [upper, lower]
    else:
        evicted = swapped(inputs, "section", mask)
        grad_in = [shifted(after(input_grad, blocks), "section", -1)]

    products = jnp.dot(after(inputs, rows_all[1:2]), flat_weight, preferred_element_type=jnp.float32)
    members = lax.axis_size("tensor")
    me = lax.axis_index("tensor")
    my_rows = rows // members
    summed = lax.dynamic_slice_in_dim(products, me * my_rows, my_rows, 0)
    for j in range(1, members):
        other = lax.dynamic_slice_in_dim(products, (me + j) % members * my_rows, my_rows, 0)
        summed = summed + shifted(other.astype(jnp.bfloat16), "tensor", j).astype(jnp.float32)
    my_positions = lax.dynamic_slice_in_dim(fwd_positions, me * my_rows, my_rows, 0)
    cosine, sine = rope_tables(my_positions, head_size)
    key_out = rotate(
        summed.reshape(my_rows, heads, head_size), cosine[:, None], sine[:, None], 1.0
    ).astype(jnp.bfloat16)

    weight_grad = lax.dot_general(
        jnp.concatenate(rows_all, 0),
        jnp.concatenate(grads_all, 0),
        (((0,), (0,)), ((), ())),
        preferred_element_type=jnp.float32,
    ).astype(jnp.bfloat16)
    weight_grad = weight_grad.reshape(share, heads, head_size)

    weight_grad = stored(weight_grad)
    first, *others = grad_in
    written = stored(first, rows)
    others, evicted = after((others, evicted), weight_grad)
    for part in others:
        written = stored(part, rows, rows // 2, into=written)
    return stored(key_out), written, stored(evicted), weight_grad


def body(fwd_input, fwd_positions, key_weight, stash, partner, key_grad, bwd_positions):
    sections = lax.axis_size("section")
    first = sections // 2
    branches = [
        lambda *blocks, mask=mask: work(mask, *blocks) for mask in range(first, sections)
    ]
    key_out, grad_in, evicted, weight_grad = lax.switch(
        partner[0] - first,
        branches,
        fwd_input[0, 0],
        fwd_positions[0, 0],
        key_weight[0],
        stash[0, 0],
        key_grad[0, 0],
        bwd_positions[0, 0],
    )
    return key_out[None, None], grad_in[None, None], evicted[None, None], weight_grad[None]


def solution(mesh):
    placed = (
        P("dp", "section", None, "tensor"),
        P("dp", "section", None),
        P("section", "tensor", None, None),
        P("dp", "section", None, "tensor"),
        P(),
        P("dp", "section", None, None, None),
        P("dp", "section", None),
    )
    return jax.shard_map(
        body,
        mesh=mesh,
        in_specs=placed,
        out_specs=(
            P("dp", "section", "tensor", None, None),
            P("dp", "section", None, "tensor"),
            P("dp", "section", None, "tensor"),
            P("section", ("tensor", "dp"), None, None),
        ),
        check_vma=False,
    )
```

```python
import functools

import jax
import jax.numpy as jnp
from jax import lax
from jax.experimental import pallas as pl
from jax.experimental.pallas import tpu as pltpu
from jax.sharding import PartitionSpec as P

THETA = 500000.0


def shifted(value, axis, distance):
    size = lax.axis_size(axis)
    return lax.ppermute(value, axis, [(i, (i + distance) % size) for i in range(size)])


def swapped(value, axis, mask):
    size = lax.axis_size(axis)
    return lax.ppermute(value, axis, [(i, i ^ mask) for i in range(size)])


def exchanged(blocks, groups=None):
    return lax.all_to_all(blocks, "dp", 0, 0, axis_index_groups=groups, tiled=True)


def after(value, earlier):
    return lax.optimization_barrier((value, earlier))[0]


def rope_tables(positions, head_size):
    half = head_size // 2
    freqs = THETA ** (-(2.0 * jnp.arange(half, dtype=jnp.float32)) / head_size)
    angles = positions.astype(jnp.float32)[..., None] * freqs
    return (jnp.cos(angles), jnp.sin(angles))


def rotate(keys, cosine, sine, sign):
    half = keys.shape[-1] // 2
    first = keys[..., :half]
    second = keys[..., half:]
    return jnp.concatenate(
        [first * cosine - sign * second * sine, second * cosine + sign * first * sine], axis=-1
    )


def store_kernel(places, *refs):
    parts, outs, sems = refs[: len(places)], refs[len(places) : -1], refs[-1]
    copies = [
        pltpu.make_async_copy(part, outs[out].at[pl.ds(row, part.shape[0])], sems.at[i])
        for i, (part, (out, row)) in enumerate(zip(parts, places))
    ]
    for copy in copies:
        copy.start()
    for copy in copies:
        copy.wait()


def stored(*groups):
    places, shapes = [], []
    for out, group in enumerate(groups):
        row = 0
        for part in group:
            places.append((out, row))
            row += part.shape[0]
        shapes.append(pltpu.HBM((row,) + group[0].shape[1:], group[0].dtype))
    parts = [pltpu.with_memory_space_constraint(part, pltpu.VMEM) for part in sum(groups, [])]
    size = sum(part.size * part.dtype.itemsize for part in parts)
    return pl.pallas_call(
        functools.partial(store_kernel, tuple(places)),
        out_shape=shapes,
        in_specs=[pl.BlockSpec(memory_space=pl.ANY)] * len(parts),
        out_specs=[pl.BlockSpec(memory_space=pl.ANY)] * len(groups),
        scratch_shapes=[pltpu.SemaphoreType.DMA((len(parts),))],
        cost_estimate=pl.CostEstimate(flops=0, bytes_accessed=2 * size, transcendentals=0),
    )(*parts)


def work(mask, inputs, fwd_positions, weight, stash, key_grad, bwd_positions):
    width, heads, head_size = weight.shape
    rows = inputs.shape[0]

    replicas = lax.axis_size("dp")
    replica = lax.axis_index("dp")
    share = width // replicas
    square = lax.axis_size("section") == 4 and replicas == 4 and mask == 2
    cut = rows // 4 if square else rows
    held = [swapped(stash[:cut], "section", mask)]
    if square:
        held.append(swapped(stash[cut:], "section", mask))

    def block_of(owner):
        start = owner * share
        return jnp.concatenate(
            [lax.dynamic_slice_in_dim(piece, start, share, 1) for piece in held]
        )

    if square:
        across = 3 - replica
        first, last = jnp.minimum(replica, across), jnp.maximum(replica, across)
        sources = [first, last, replica ^ 1, replica ^ 2]
        blocks = [block_of(owner) for owner in sources]
        pair = exchanged(jnp.stack(blocks[:2]), [[0, 3], [1, 2]])
        rows_all = [pair[0], pair[1]] + [swapped(blocks[1 + j], "dp", j) for j in (1, 2)]
    else:
        sources = [(replica - j) % replicas for j in range(replicas)]
        blocks = [block_of((replica + j) % replicas) for j in range(replicas)]
        rows_all = [shifted(block, "dp", j) if j else block for j, block in enumerate(blocks)]
    flat_weight = weight.reshape(width, heads * head_size)

    back_cos, back_sin = rope_tables(bwd_positions, head_size)
    grad_pre = rotate(
        key_grad.astype(jnp.float32), back_cos[:, None], back_sin[:, None], -1.0
    ).astype(jnp.bfloat16)
    grad_flat = grad_pre.reshape(rows, heads * head_size)
    grads_all = exchanged(jnp.broadcast_to(grad_flat, (replicas, *grad_flat.shape)))
    grads_all = [
        lax.dynamic_index_in_dim(grads_all, source, 0, keepdims=False) for source in sources
    ]

    input_grad = jnp.einsum(
        "rn,dn->rd", grad_flat, flat_weight, preferred_element_type=jnp.float32
    ).astype(jnp.bfloat16)
    if square:
        half = rows // 2
        lower, ahead = after((input_grad[half:], inputs), held[0])
        turned = lax.ppermute(lower, "section", [(0, 2), (2, 0)])
        evicted = swapped(ahead, "section", mask)
        odd = lax.axis_index("section") % 2 == 1
        lower = swapped(jnp.where(odd, lower, after(turned, blocks)), "section", 1)
        upper = shifted(after(input_grad[:half], blocks), "section", -1)
        grad_in = [upper, lower]
    else:
        evicted = swapped(inputs, "section", mask)
        grad_in = [shifted(after(input_grad, blocks), "section", -1)]

    products = jnp.dot(
        after(inputs, rows_all[-1] if square else rows_all[1]),
        flat_weight,
        preferred_element_type=jnp.float32,
    )
    members = lax.axis_size("tensor")
    me = lax.axis_index("tensor")
    my_rows = rows // members
    summed = lax.dynamic_slice_in_dim(products, me * my_rows, my_rows, 0)
    for j in range(1, members):
        other = lax.dynamic_slice_in_dim(products, (me + j) % members * my_rows, my_rows, 0)
        summed = summed + shifted(other.astype(jnp.bfloat16), "tensor", j).astype(jnp.float32)
    my_positions = lax.dynamic_slice_in_dim(fwd_positions, me * my_rows, my_rows, 0)
    cosine, sine = rope_tables(my_positions, head_size)
    key_out = rotate(
        summed.reshape(my_rows, heads, head_size), cosine[:, None], sine[:, None], 1.0
    ).astype(jnp.bfloat16)

    weight_grad = lax.dot_general(
        jnp.concatenate(rows_all, 0),
        jnp.concatenate(grads_all, 0),
        (((0,), (0,)), ((), ())),
        preferred_element_type=jnp.float32,
    ).astype(jnp.bfloat16)
    weight_grad = weight_grad.reshape(share, heads, head_size)

    key_out, weight_grad = stored([key_out], [weight_grad])
    grad_in, evicted = after((grad_in, evicted), weight_grad)
    if square:
        grad_in, evicted = stored(grad_in, [evicted])
    else:
        (evicted,) = stored([evicted])
        (grad_in,) = stored(grad_in)
    return key_out, grad_in, evicted, weight_grad


def body(fwd_input, fwd_positions, key_weight, stash, partner, key_grad, bwd_positions):
    sections = lax.axis_size("section")
    first = sections // 2
    branches = [
        lambda *blocks, mask=mask: work(mask, *blocks) for mask in range(first, sections)
    ]
    key_out, grad_in, evicted, weight_grad = lax.switch(
        partner[0] - first,
        branches,
        fwd_input[0, 0],
        fwd_positions[0, 0],
        key_weight[0],
        stash[0, 0],
        key_grad[0, 0],
        bwd_positions[0, 0],
    )
    return key_out[None, None], grad_in[None, None], evicted[None, None], weight_grad[None]


def solution(mesh):
    placed = (
        P("dp", "section", None, "tensor"),
        P("dp", "section", None),
        P("section", "tensor", None, None),
        P("dp", "section", None, "tensor"),
        P(),
        P("dp", "section", None, None, None),
        P("dp", "section", None),
    )
    return jax.shard_map(
        body,
        mesh=mesh,
        in_specs=placed,
        out_specs=(
            P("dp", "section", "tensor", None, None),
            P("dp", "section", None, "tensor"),
            P("dp", "section", None, "tensor"),
            P("section", ("tensor", "dp"), None, None),
        ),
        check_vma=False,
    )
```

```python
import functools

import jax
import jax.numpy as jnp
from jax import lax
from jax.experimental import pallas as pl
from jax.experimental.pallas import tpu as pltpu
from jax.sharding import PartitionSpec as P

THETA = 500000.0


def shifted(value, axis, distance):
    size = lax.axis_size(axis)
    return lax.ppermute(value, axis, [(i, (i + distance) % size) for i in range(size)])


def swapped(value, axis, mask):
    size = lax.axis_size(axis)
    return lax.ppermute(value, axis, [(i, i ^ mask) for i in range(size)])


def exchanged(blocks, groups=None):
    return lax.all_to_all(blocks, "dp", 0, 0, axis_index_groups=groups, tiled=True)


def after(value, earlier):
    return lax.optimization_barrier((value, earlier))[0]


def rope_tables(positions, head_size):
    half = head_size // 2
    freqs = THETA ** (-(2.0 * jnp.arange(half, dtype=jnp.float32)) / head_size)
    angles = positions.astype(jnp.float32)[..., None] * freqs
    return (jnp.cos(angles), jnp.sin(angles))


def rotate(keys, cosine, sine, sign):
    half = keys.shape[-1] // 2
    first = keys[..., :half]
    second = keys[..., half:]
    return jnp.concatenate(
        [first * cosine - sign * second * sine, second * cosine + sign * first * sine], axis=-1
    )


def store_kernel(places, *refs):
    parts, outs, sems = refs[: len(places)], refs[len(places) : -1], refs[-1]
    copies = [
        pltpu.make_async_copy(part, outs[out].at[pl.ds(row, part.shape[0])], sems.at[i])
        for i, (part, (out, row)) in enumerate(zip(parts, places))
    ]
    for copy in copies:
        copy.start()
    for copy in copies:
        copy.wait()


def stored(*groups):
    places, shapes = [], []
    for out, group in enumerate(groups):
        row = 0
        for part in group:
            places.append((out, row))
            row += part.shape[0]
        shapes.append(pltpu.HBM((row,) + group[0].shape[1:], group[0].dtype))
    parts = [pltpu.with_memory_space_constraint(part, pltpu.VMEM) for part in sum(groups, [])]
    size = sum(part.size * part.dtype.itemsize for part in parts)
    return pl.pallas_call(
        functools.partial(store_kernel, tuple(places)),
        out_shape=shapes,
        in_specs=[pl.BlockSpec(memory_space=pl.ANY)] * len(parts),
        out_specs=[pl.BlockSpec(memory_space=pl.ANY)] * len(groups),
        scratch_shapes=[pltpu.SemaphoreType.DMA((len(parts),))],
        cost_estimate=pl.CostEstimate(flops=0, bytes_accessed=2 * size, transcendentals=0),
        compiler_params=pltpu.CompilerParams(vmem_limit_bytes=1 << 20),
    )(*parts)


def work(mask, inputs, fwd_positions, weight, stash, key_grad, bwd_positions):
    width, heads, head_size = weight.shape
    rows = inputs.shape[0]

    replicas = lax.axis_size("dp")
    replica = lax.axis_index("dp")
    share = width // replicas
    square = lax.axis_size("section") == 4 and mask == 2
    cut = rows // 4 if square else rows
    held = [swapped(stash[:cut], "section", mask)]
    if square:
        held.append(swapped(stash[cut:], "section", mask))

    def block_of(owner):
        start = owner * share
        return jnp.concatenate(
            [lax.dynamic_slice_in_dim(piece, start, share, 1) for piece in held]
        )

    blocks = [block_of((replica + j) % replicas) for j in range(replicas)]
    flat_weight = weight.reshape(width, heads * head_size)

    back_cos, back_sin = rope_tables(bwd_positions, head_size)
    grad_pre = rotate(
        key_grad.astype(jnp.float32), back_cos[:, None], back_sin[:, None], -1.0
    ).astype(jnp.bfloat16)
    grad_flat = grad_pre.reshape(rows, heads * head_size)
    copies = jnp.broadcast_to(grad_flat, (replicas, *grad_flat.shape))
    grads_all = exchanged(after(copies, held[0]) if square else copies)
    grads_all = [
        lax.dynamic_index_in_dim(grads_all, (replica - j) % replicas, 0, keepdims=False)
        for j in range(replicas)
    ]

    input_grad = jnp.einsum(
        "rn,dn->rd", grad_flat, flat_weight, preferred_element_type=jnp.float32
    ).astype(jnp.bfloat16)
    if square:
        half = rows // 2
        upper, lower, ahead = after((input_grad[:half], input_grad[half:], inputs), held[0])
        odd = lax.axis_index("section") % 2 == 1
        upper = swapped(upper, "section", 1)
        lower_by_2 = lax.ppermute(lower, "section", [(0, 2), (2, 0)])
        evicted = swapped(ahead, "section", mask)
        upper_by_2 = lax.ppermute(after(upper, blocks), "section", [(1, 3), (3, 1)])
        lower = swapped(jnp.where(odd, lower, after(lower_by_2, blocks)), "section", 1)
        grad_in = [jnp.where(odd, upper_by_2, upper), lower]
        blocks[-1] = after(blocks[-1], upper)
    else:
        evicted = swapped(inputs, "section", mask)
        grad_in = [shifted(after(input_grad, blocks), "section", -1)]

    rows_all = [shifted(block, "dp", j) if j else block for j, block in enumerate(blocks)]

    products = jnp.dot(
        after(inputs, rows_all[1]),
        flat_weight,
        preferred_element_type=jnp.float32,
    )
    members = lax.axis_size("tensor")
    me = lax.axis_index("tensor")
    my_rows = rows // members
    summed = lax.dynamic_slice_in_dim(products, me * my_rows, my_rows, 0)
    for j in range(1, members):
        other = lax.dynamic_slice_in_dim(products, (me + j) % members * my_rows, my_rows, 0)
        summed = summed + shifted(other.astype(jnp.bfloat16), "tensor", j).astype(jnp.float32)
    my_positions = lax.dynamic_slice_in_dim(fwd_positions, me * my_rows, my_rows, 0)
    cosine, sine = rope_tables(my_positions, head_size)
    key_out = rotate(
        summed.reshape(my_rows, heads, head_size), cosine[:, None], sine[:, None], 1.0
    ).astype(jnp.bfloat16)

    weight_grad = lax.dot_general(
        jnp.concatenate(rows_all, 0),
        jnp.concatenate(grads_all, 0),
        (((0,), (0,)), ((), ())),
        preferred_element_type=jnp.float32,
    ).astype(jnp.bfloat16)
    weight_grad = weight_grad.reshape(share, heads, head_size)

    (weight_grad,) = stored([weight_grad])
    grad_in, evicted = after((grad_in, evicted), weight_grad)
    if square:
        key_out, grad_in, evicted = stored([key_out], grad_in, [evicted])
    else:
        key_out, evicted = stored([key_out], [evicted])
        (grad_in,) = stored(after(grad_in, evicted))
    return key_out, grad_in, evicted, weight_grad


def body(fwd_input, fwd_positions, key_weight, stash, partner, key_grad, bwd_positions):
    sections = lax.axis_size("section")
    first = sections // 2
    branches = [
        lambda *blocks, mask=mask: work(mask, *blocks) for mask in range(first, sections)
    ]
    key_out, grad_in, evicted, weight_grad = lax.switch(
        partner[0] - first,
        branches,
        fwd_input[0, 0],
        fwd_positions[0, 0],
        key_weight[0],
        stash[0, 0],
        key_grad[0, 0],
        bwd_positions[0, 0],
    )
    return key_out[None, None], grad_in[None, None], evicted[None, None], weight_grad[None]


def solution(mesh):
    placed = (
        P("dp", "section", None, "tensor"),
        P("dp", "section", None),
        P("section", "tensor", None, None),
        P("dp", "section", None, "tensor"),
        P(),
        P("dp", "section", None, None, None),
        P("dp", "section", None),
    )
    return jax.shard_map(
        body,
        mesh=mesh,
        in_specs=placed,
        out_specs=(
            P("dp", "section", "tensor", None, None),
            P("dp", "section", None, "tensor"),
            P("dp", "section", None, "tensor"),
            P("section", ("tensor", "dp"), None, None),
        ),
        check_vma=False,
    )
```

```python
import functools

import jax
import jax.numpy as jnp
from jax import lax
from jax.experimental import pallas as pl
from jax.experimental.pallas import tpu as pltpu
from jax.sharding import PartitionSpec as P

THETA = 500000.0


def shifted(value, axis, distance):
    size = lax.axis_size(axis)
    return lax.ppermute(value, axis, [(i, (i + distance) % size) for i in range(size)])


def swapped(value, axis, mask):
    size = lax.axis_size(axis)
    return lax.ppermute(value, axis, [(i, i ^ mask) for i in range(size)])


def exchanged(blocks, groups=None):
    return lax.all_to_all(blocks, "dp", 0, 0, axis_index_groups=groups, tiled=True)


def after(value, earlier):
    return lax.optimization_barrier((value, earlier))[0]


def rope_tables(positions, head_size):
    half = head_size // 2
    freqs = THETA ** (-(2.0 * jnp.arange(half, dtype=jnp.float32)) / head_size)
    angles = positions.astype(jnp.float32)[..., None] * freqs
    return (jnp.cos(angles), jnp.sin(angles))


def rotate(keys, cosine, sine, sign):
    half = keys.shape[-1] // 2
    first = keys[..., :half]
    second = keys[..., half:]
    return jnp.concatenate(
        [first * cosine - sign * second * sine, second * cosine + sign * first * sine], axis=-1
    )


def store_kernel(places, *refs):
    parts, outs, sems = refs[: len(places)], refs[len(places) : -1], refs[-1]
    copies = [
        pltpu.make_async_copy(part, outs[out].at[pl.ds(row, part.shape[0])], sems.at[i])
        for i, (part, (out, row)) in enumerate(zip(parts, places))
    ]
    for copy in copies:
        copy.start()
    for copy in copies:
        copy.wait()


def stored(*groups):
    places, shapes = [], []
    for out, group in enumerate(groups):
        row = 0
        for part in group:
            places.append((out, row))
            row += part.shape[0]
        shapes.append(pltpu.HBM((row,) + group[0].shape[1:], group[0].dtype))
    parts = [pltpu.with_memory_space_constraint(part, pltpu.VMEM) for part in sum(groups, [])]
    size = sum(part.size * part.dtype.itemsize for part in parts)
    return pl.pallas_call(
        functools.partial(store_kernel, tuple(places)),
        out_shape=shapes,
        in_specs=[pl.BlockSpec(memory_space=pl.ANY)] * len(parts),
        out_specs=[pl.BlockSpec(memory_space=pl.ANY)] * len(groups),
        scratch_shapes=[pltpu.SemaphoreType.DMA((len(parts),))],
        cost_estimate=pl.CostEstimate(flops=0, bytes_accessed=2 * size, transcendentals=0),
        compiler_params=pltpu.CompilerParams(vmem_limit_bytes=1 << 20),
    )(*parts)


def product_kernel(*refs):
    count = (len(refs) - 3) // 2
    lefts, rights = refs[:count], refs[count : 2 * count]
    out, buffer, sems = refs[2 * count :]
    steps, step, heads, _ = buffer.shape
    copies = []
    for i in range(steps):
        total = sum(
            lax.dot_general(
                left[:, i * step : (i + 1) * step],
                right[...],
                (((0,), (0,)), ((), ())),
                preferred_element_type=jnp.float32,
            )
            for left, right in zip(lefts, rights)
        )
        buffer[i] = pltpu.einshape("a(bc)->abc", total, b=heads).astype(out.dtype)
        copies.append(
            pltpu.make_async_copy(buffer.at[i], out.at[pl.ds(i * step, step)], sems.at[i])
        )
        copies[-1].start()
    for copy in copies:
        copy.wait()


def summed_products(lefts, rights, heads):
    rows, depth = lefts[0].shape[1], lefts[0].shape[0]
    columns = rights[0].shape[1]
    steps = 4 if rows % 1024 == 0 else 1
    shape = (rows, heads, columns // heads)
    return pl.pallas_call(
        product_kernel,
        out_shape=pltpu.HBM(shape, lefts[0].dtype),
        in_specs=[pl.BlockSpec(memory_space=pltpu.VMEM)] * (2 * len(lefts)),
        out_specs=pl.BlockSpec(memory_space=pl.ANY),
        scratch_shapes=[
            pltpu.VMEM((steps, rows // steps) + shape[1:], lefts[0].dtype),
            pltpu.SemaphoreType.DMA((steps,)),
        ],
        cost_estimate=pl.CostEstimate(
            flops=2 * len(lefts) * depth * rows * columns,
            bytes_accessed=4 * rows * columns,
            transcendentals=0,
        ),
        compiler_params=pltpu.CompilerParams(vmem_limit_bytes=16 << 20),
    )(*lefts, *rights)


def work(mask, inputs, fwd_positions, weight, stash, key_grad, bwd_positions):
    width, heads, head_size = weight.shape
    rows = inputs.shape[0]

    replicas = lax.axis_size("dp")
    replica = lax.axis_index("dp")
    share = width // replicas
    square = lax.axis_size("section") == 4 and mask == 2
    cut = rows // 4 if square else rows
    held = [swapped(stash[:cut], "section", mask)]
    if square:
        held.append(swapped(stash[cut:], "section", mask))

    def block_of(owner):
        start = owner * share
        return jnp.concatenate(
            [lax.dynamic_slice_in_dim(piece, start, share, 1) for piece in held]
        )

    blocks = [block_of((replica + j) % replicas) for j in range(replicas)]
    flat_weight = weight.reshape(width, heads * head_size)

    back_cos, back_sin = rope_tables(bwd_positions, head_size)
    grad_pre = rotate(
        key_grad.astype(jnp.float32), back_cos[:, None], back_sin[:, None], -1.0
    ).astype(jnp.bfloat16)
    grad_flat = grad_pre.reshape(rows, heads * head_size)
    copies = jnp.broadcast_to(grad_flat, (replicas, *grad_flat.shape))
    grads_all = exchanged(after(copies, held[0]) if square else copies)
    grads_all = [
        lax.dynamic_index_in_dim(grads_all, (replica - j) % replicas, 0, keepdims=False)
        for j in range(replicas)
    ]

    input_grad = jnp.einsum(
        "rn,dn->rd", grad_flat, flat_weight, preferred_element_type=jnp.float32
    ).astype(jnp.bfloat16)
    if square:
        half = rows // 2
        upper, lower, ahead = after((input_grad[:half], input_grad[half:], inputs), held[0])
        odd = lax.axis_index("section") % 2 == 1
        upper = swapped(upper, "section", 1)
        lower_by_2 = lax.ppermute(lower, "section", [(0, 2), (2, 0)])
        evicted = swapped(ahead, "section", mask)
        upper_by_2 = lax.ppermute(after(upper, blocks), "section", [(1, 3), (3, 1)])
        lower = swapped(jnp.where(odd, lower, after(lower_by_2, blocks)), "section", 1)
        grad_in = [jnp.where(odd, upper_by_2, upper), lower]
        blocks[-1] = after(blocks[-1], upper)
    else:
        evicted = swapped(inputs, "section", mask)
        grad_in = [shifted(after(input_grad, blocks), "section", -1)]

    rows_all = [shifted(block, "dp", j) if j else block for j, block in enumerate(blocks)]

    products = jnp.dot(
        after(inputs, rows_all[1]),
        flat_weight,
        preferred_element_type=jnp.float32,
    )
    members = lax.axis_size("tensor")
    me = lax.axis_index("tensor")
    my_rows = rows // members
    summed = lax.dynamic_slice_in_dim(products, me * my_rows, my_rows, 0)
    for j in range(1, members):
        other = lax.dynamic_slice_in_dim(products, (me + j) % members * my_rows, my_rows, 0)
        summed = summed + shifted(other.astype(jnp.bfloat16), "tensor", j).astype(jnp.float32)
    my_positions = lax.dynamic_slice_in_dim(fwd_positions, me * my_rows, my_rows, 0)
    cosine, sine = rope_tables(my_positions, head_size)
    key_out = rotate(
        summed.reshape(my_rows, heads, head_size), cosine[:, None], sine[:, None], 1.0
    ).astype(jnp.bfloat16)

    weight_grad = summed_products(
        [jnp.concatenate(rows_all, 0)], [jnp.concatenate(grads_all, 0)], heads
    )
    grad_in, evicted = after((grad_in, evicted), weight_grad)
    if square:
        key_out, grad_in, evicted = stored([key_out], grad_in, [evicted])
    else:
        key_out, evicted = stored([key_out], [evicted])
        (grad_in,) = stored(after(grad_in, evicted))
    return key_out, grad_in, evicted, weight_grad


def body(fwd_input, fwd_positions, key_weight, stash, partner, key_grad, bwd_positions):
    sections = lax.axis_size("section")
    first = sections // 2
    branches = [
        lambda *blocks, mask=mask: work(mask, *blocks) for mask in range(first, sections)
    ]
    key_out, grad_in, evicted, weight_grad = lax.switch(
        partner[0] - first,
        branches,
        fwd_input[0, 0],
        fwd_positions[0, 0],
        key_weight[0],
        stash[0, 0],
        key_grad[0, 0],
        bwd_positions[0, 0],
    )
    return key_out[None, None], grad_in[None, None], evicted[None, None], weight_grad[None]


def solution(mesh):
    placed = (
        P("dp", "section", None, "tensor"),
        P("dp", "section", None),
        P("section", "tensor", None, None),
        P("dp", "section", None, "tensor"),
        P(),
        P("dp", "section", None, None, None),
        P("dp", "section", None),
    )
    return jax.shard_map(
        body,
        mesh=mesh,
        in_specs=placed,
        out_specs=(
            P("dp", "section", "tensor", None, None),
            P("dp", "section", None, "tensor"),
            P("dp", "section", None, "tensor"),
            P("section", ("tensor", "dp"), None, None),
        ),
        check_vma=False,
    )
```

```python
import functools

import jax
import jax.numpy as jnp
from jax import lax
from jax.experimental import pallas as pl
from jax.experimental.pallas import tpu as pltpu
from jax.sharding import PartitionSpec as P

THETA = 500000.0


def shifted(value, axis, distance):
    size = lax.axis_size(axis)
    return lax.ppermute(value, axis, [(i, (i + distance) % size) for i in range(size)])


def swapped(value, axis, mask):
    size = lax.axis_size(axis)
    return lax.ppermute(value, axis, [(i, i ^ mask) for i in range(size)])


def exchanged(blocks, groups=None):
    return lax.all_to_all(blocks, "dp", 0, 0, axis_index_groups=groups, tiled=True)


def after(value, earlier):
    return lax.optimization_barrier((value, earlier))[0]


def rope_tables(positions, head_size):
    half = head_size // 2
    freqs = THETA ** (-(2.0 * jnp.arange(half, dtype=jnp.float32)) / head_size)
    angles = positions.astype(jnp.float32)[..., None] * freqs
    return (jnp.cos(angles), jnp.sin(angles))


def rotate(keys, cosine, sine, sign):
    half = keys.shape[-1] // 2
    first = keys[..., :half]
    second = keys[..., half:]
    return jnp.concatenate(
        [first * cosine - sign * second * sine, second * cosine + sign * first * sine], axis=-1
    )


def store_kernel(places, *refs):
    outs = max(out for out, _, _ in places) + 1
    parts, outs, sems = refs[: -1 - outs], refs[-1 - outs : -1], refs[-1]
    parts = list(parts)
    copies = []
    for i, (out, row, choice) in enumerate(places):
        part = parts.pop(0)
        rows = outs[out].at[pl.ds(row, part.shape[0])]
        copies.append(pltpu.make_async_copy(part, rows, sems.at[i]))
        if choice:
            other = pltpu.make_async_copy(parts.pop(0), rows, sems.at[i])
            odd = lax.axis_index("section") % 2 == 1
            pl.when(odd)(other.start)
            pl.when(jnp.logical_not(odd))(copies[i].start)
        else:
            copies[i].start()
    for copy in copies:
        copy.wait()


def stored(*groups):
    places, shapes, parts = [], [], []
    for out, group in enumerate(groups):
        row = 0
        for part in group:
            choice = isinstance(part, tuple)
            parts.extend(part if choice else [part])
            places.append((out, row, choice))
            row += parts[-1].shape[0]
        shapes.append(pltpu.HBM((row,) + parts[-1].shape[1:], parts[-1].dtype))
    parts = [pltpu.with_memory_space_constraint(part, pltpu.VMEM) for part in parts]
    size = sum(part.size * part.dtype.itemsize for part in parts)
    return pl.pallas_call(
        functools.partial(store_kernel, tuple(places)),
        out_shape=shapes,
        in_specs=[pl.BlockSpec(memory_space=pl.ANY)] * len(parts),
        out_specs=[pl.BlockSpec(memory_space=pl.ANY)] * len(groups),
        scratch_shapes=[pltpu.SemaphoreType.DMA((len(places),))],
        cost_estimate=pl.CostEstimate(flops=0, bytes_accessed=2 * size, transcendentals=0),
        compiler_params=pltpu.CompilerParams(vmem_limit_bytes=1 << 20),
    )(*parts)


def product_kernel(count, *refs):
    lefts, rights, refs = refs[:count], refs[count : 2 * count], refs[2 * count :]
    copies = []
    if len(refs) == 3:
        out, buffer, sems = refs
    else:
        array, out, array_out, buffer, sems = refs
        copies.append(pltpu.make_async_copy(array, array_out, sems.at[buffer.shape[0]]))
        copies[0].start()
    steps, step, heads, _ = buffer.shape
    for i in range(steps):
        total = sum(
            lax.dot_general(
                left[:, i * step : (i + 1) * step],
                right[...],
                (((0,), (0,)), ((), ())),
                preferred_element_type=jnp.float32,
            )
            for left, right in zip(lefts, rights)
        )
        buffer[i] = pltpu.einshape("a(bc)->abc", total, b=heads).astype(out.dtype)
        copies.append(
            pltpu.make_async_copy(buffer.at[i], out.at[pl.ds(i * step, step)], sems.at[i])
        )
        copies[-1].start()
    for copy in copies:
        copy.wait()


def summed_products(lefts, rights, heads, array=None):
    rows, columns = lefts[0].shape[1], rights[0].shape[1]
    steps = 4 if rows % 1024 == 0 else 1
    kind = lefts[0].dtype
    shape = (rows, heads, columns // heads)
    shapes, operands = [pltpu.HBM(shape, kind)], [*lefts, *rights]
    specs = [pl.BlockSpec(memory_space=pltpu.VMEM)] * len(operands)
    if array is not None:
        shapes.append(pltpu.HBM(array.shape, array.dtype))
        operands.append(pltpu.with_memory_space_constraint(array, pltpu.VMEM))
        specs.append(pl.BlockSpec(memory_space=pl.ANY))
    return pl.pallas_call(
        functools.partial(product_kernel, len(lefts)),
        out_shape=shapes,
        in_specs=specs,
        out_specs=[pl.BlockSpec(memory_space=pl.ANY)] * len(shapes),
        scratch_shapes=[
            pltpu.VMEM((steps, rows // steps) + shape[1:], kind),
            pltpu.SemaphoreType.DMA((steps + 1,)),
        ],
        cost_estimate=pl.CostEstimate(
            flops=2 * sum(left.size for left in lefts) * columns,
            bytes_accessed=4 * rows * columns,
            transcendentals=0,
        ),
        compiler_params=pltpu.CompilerParams(vmem_limit_bytes=16 << 20),
    )(*operands)


def work(mask, inputs, fwd_positions, weight, stash, key_grad, bwd_positions):
    width, heads, head_size = weight.shape
    rows = inputs.shape[0]

    replicas = lax.axis_size("dp")
    replica = lax.axis_index("dp")
    share = width // replicas
    square = lax.axis_size("section") == 4 and mask == 2
    cut = rows // 4 if square else rows
    held = [swapped(stash[:cut], "section", mask)]
    if square:
        held.append(swapped(stash[cut:], "section", mask))

    def block_of(owner):
        start = owner * share
        return jnp.concatenate(
            [lax.dynamic_slice_in_dim(piece, start, share, 1) for piece in held]
        )

    blocks = [block_of((replica + j) % replicas) for j in range(replicas)]
    flat_weight = weight.reshape(width, heads * head_size)

    back_cos, back_sin = rope_tables(bwd_positions, head_size)
    grad_pre = rotate(
        key_grad.astype(jnp.float32), back_cos[:, None], back_sin[:, None], -1.0
    ).astype(jnp.bfloat16)
    grad_flat = grad_pre.reshape(rows, heads * head_size)
    copies = jnp.broadcast_to(grad_flat, (replicas, *grad_flat.shape))
    grads_all = exchanged(after(copies, held[0]) if square else copies)
    grads_all = [
        lax.dynamic_index_in_dim(grads_all, (replica - j) % replicas, 0, keepdims=False)
        for j in range(replicas)
    ]

    input_grad = jnp.einsum(
        "rn,dn->rd", grad_flat, flat_weight, preferred_element_type=jnp.float32
    ).astype(jnp.bfloat16)
    if square:
        half = rows // 2
        upper, lower, ahead = after((input_grad[:half], input_grad[half:], inputs), held[0])
        odd = lax.axis_index("section") % 2 == 1
        upper = swapped(upper, "section", 1)
        lower_by_2 = lax.ppermute(lower, "section", [(0, 2), (2, 0)])
        evicted = swapped(ahead, "section", mask)
        upper_by_2 = lax.ppermute(after(upper, blocks), "section", [(1, 3), (3, 1)])
        lower = swapped(jnp.where(odd, lower, after(lower_by_2, blocks)), "section", 1)
        grad_in = [(upper, upper_by_2), lower]
        blocks[-1] = after(blocks[-1], upper)
    else:
        evicted = swapped(inputs, "section", mask)
        grad_in = [shifted(after(input_grad, blocks), "section", -1)]

    rows_all = [shifted(block, "dp", j) if j else block for j, block in enumerate(blocks)]

    products = jnp.dot(
        after(inputs, rows_all[1]),
        flat_weight,
        preferred_element_type=jnp.float32,
    )
    members = lax.axis_size("tensor")
    me = lax.axis_index("tensor")
    my_rows = rows // members
    summed = lax.dynamic_slice_in_dim(products, me * my_rows, my_rows, 0)
    for j in range(1, members):
        other = lax.dynamic_slice_in_dim(products, (me + j) % members * my_rows, my_rows, 0)
        summed = summed + shifted(other.astype(jnp.bfloat16), "tensor", j).astype(jnp.float32)
    my_positions = lax.dynamic_slice_in_dim(fwd_positions, me * my_rows, my_rows, 0)
    cosine, sine = rope_tables(my_positions, head_size)
    key_out = rotate(
        summed.reshape(my_rows, heads, head_size), cosine[:, None], sine[:, None], 1.0
    ).astype(jnp.bfloat16)

    lefts = [jnp.concatenate(rows_all[:-1], 0), rows_all[-1]]
    rights = [jnp.concatenate(grads_all[:-1], 0), grads_all[-1]]
    if square:
        (weight_grad,) = summed_products(lefts, rights, heads)
        grad_in, evicted = after((grad_in, evicted), weight_grad)
        key_out, grad_in, evicted = stored([key_out], grad_in, [evicted])
    else:
        weight_grad, evicted = summed_products(lefts, rights, heads, evicted)
        key_out, grad_in = stored([key_out], grad_in)
    return key_out, grad_in, evicted, weight_grad


def body(fwd_input, fwd_positions, key_weight, stash, partner, key_grad, bwd_positions):
    sections = lax.axis_size("section")
    first = sections // 2
    branches = [
        lambda *blocks, mask=mask: work(mask, *blocks) for mask in range(first, sections)
    ]
    key_out, grad_in, evicted, weight_grad = lax.switch(
        partner[0] - first,
        branches,
        fwd_input[0, 0],
        fwd_positions[0, 0],
        key_weight[0],
        stash[0, 0],
        key_grad[0, 0],
        bwd_positions[0, 0],
    )
    return key_out[None, None], grad_in[None, None], evicted[None, None], weight_grad[None]


def solution(mesh):
    placed = (
        P("dp", "section", None, "tensor"),
        P("dp", "section", None),
        P("section", "tensor", None, None),
        P("dp", "section", None, "tensor"),
        P(),
        P("dp", "section", None, None, None),
        P("dp", "section", None),
    )
    return jax.shard_map(
        body,
        mesh=mesh,
        in_specs=placed,
        out_specs=(
            P("dp", "section", "tensor", None, None),
            P("dp", "section", None, "tensor"),
            P("dp", "section", None, "tensor"),
            P("section", ("tensor", "dp"), None, None),
        ),
        check_vma=False,
    )
```

```python
import functools

import jax
import jax.numpy as jnp
from jax import lax
from jax.experimental import pallas as pl
from jax.experimental.pallas import tpu as pltpu
from jax.sharding import PartitionSpec as P

THETA = 500000.0


def shifted(value, axis, distance):
    size = lax.axis_size(axis)
    return lax.ppermute(value, axis, [(i, (i + distance) % size) for i in range(size)])


def swapped(value, axis, mask):
    size = lax.axis_size(axis)
    return lax.ppermute(value, axis, [(i, i ^ mask) for i in range(size)])


def exchanged(blocks, groups=None):
    return lax.all_to_all(blocks, "dp", 0, 0, axis_index_groups=groups, tiled=True)


def after(value, earlier):
    return lax.optimization_barrier((value, earlier))[0]


def rope_tables(positions, head_size):
    half = head_size // 2
    freqs = THETA ** (-(2.0 * jnp.arange(half, dtype=jnp.float32)) / head_size)
    angles = positions.astype(jnp.float32)[..., None] * freqs
    return (jnp.cos(angles), jnp.sin(angles))


def rotate(keys, cosine, sine, sign):
    half = keys.shape[-1] // 2
    first = keys[..., :half]
    second = keys[..., half:]
    return jnp.concatenate(
        [first * cosine - sign * second * sine, second * cosine + sign * first * sine], axis=-1
    )


def store_kernel(places, patched, *refs):
    outs = max(out for out, _, _ in places) + 1
    parts, outs, sems = list(refs[: -1 - outs]), refs[-1 - outs : -1], refs[-1]
    section = lax.axis_index("section")
    odd = section % 2 == 1
    copies = []
    for i, (out, row, choice) in enumerate(places):
        part = parts.pop(0)
        rows = outs[out].at[pl.ds(row, part.shape[0])]
        copies.append(pltpu.make_async_copy(part, rows, sems.at[i]))
        if choice:
            other = pltpu.make_async_copy(parts.pop(0), rows, sems.at[i])
            pl.when(odd)(other.start)
            pl.when(jnp.logical_not(odd))(copies[i].start)
        elif patched is None or out < len(outs) - 1:
            copies[i].start()
        else:
            pl.when(section == patched)(copies[i].start)
    for i, copy in enumerate(copies):
        if patched is None or i < len(copies) - 1:
            copy.wait()
        else:
            pl.when(section == patched)(copy.wait)


def stored(*groups, patched=None, into=None):
    places, shapes, parts = [], [], []
    for out, group in enumerate(groups):
        row = 0
        for part in group:
            choice = isinstance(part, tuple)
            parts.extend(part if choice else [part])
            places.append((out, row, choice))
            row += parts[-1].shape[0]
        shapes.append(pltpu.HBM((row,) + parts[-1].shape[1:], parts[-1].dtype))
    parts = [pltpu.with_memory_space_constraint(part, pltpu.VMEM) for part in parts]
    size = sum(part.size * part.dtype.itemsize for part in parts)
    aliases = {}
    if into is not None:
        aliases = {len(parts): len(groups) - 1}
        parts.append(pltpu.with_memory_space_constraint(into, pltpu.HBM))
    return pl.pallas_call(
        functools.partial(store_kernel, tuple(places), patched),
        out_shape=shapes,
        in_specs=[pl.BlockSpec(memory_space=pl.ANY)] * len(parts),
        out_specs=[pl.BlockSpec(memory_space=pl.ANY)] * len(groups),
        scratch_shapes=[pltpu.SemaphoreType.DMA((len(places),))],
        input_output_aliases=aliases,
        cost_estimate=pl.CostEstimate(flops=0, bytes_accessed=2 * size, transcendentals=0),
        compiler_params=pltpu.CompilerParams(vmem_limit_bytes=1 << 20),
    )(*parts)


def product_kernel(count, *refs):
    lefts, rights, refs = refs[:count], refs[count : 2 * count], refs[2 * count :]
    copies = []
    if len(refs) == 3:
        out, buffer, sems = refs
    else:
        array, out, array_out, buffer, sems = refs
        copies.append(pltpu.make_async_copy(array, array_out, sems.at[buffer.shape[0]]))
        copies[0].start()
    steps, step, heads, _ = buffer.shape
    for i in range(steps):
        total = sum(
            lax.dot_general(
                left[:, i * step : (i + 1) * step],
                right[...],
                (((0,), (0,)), ((), ())),
                preferred_element_type=jnp.float32,
            )
            for left, right in zip(lefts, rights)
        )
        buffer[i] = pltpu.einshape("a(bc)->abc", total, b=heads).astype(out.dtype)
        copies.append(
            pltpu.make_async_copy(buffer.at[i], out.at[pl.ds(i * step, step)], sems.at[i])
        )
        copies[-1].start()
    for copy in copies:
        copy.wait()


def summed_products(lefts, rights, heads, array=None):
    rows, columns = lefts[0].shape[1], rights[0].shape[1]
    steps = 4 if rows % 1024 == 0 else 1
    kind = lefts[0].dtype
    shape = (rows, heads, columns // heads)
    shapes, operands = [pltpu.HBM(shape, kind)], [*lefts, *rights]
    specs = [pl.BlockSpec(memory_space=pltpu.VMEM)] * len(operands)
    if array is not None:
        shapes.append(pltpu.HBM(array.shape, array.dtype))
        operands.append(pltpu.with_memory_space_constraint(array, pltpu.VMEM))
        specs.append(pl.BlockSpec(memory_space=pl.ANY))
    return pl.pallas_call(
        functools.partial(product_kernel, len(lefts)),
        out_shape=shapes,
        in_specs=specs,
        out_specs=[pl.BlockSpec(memory_space=pl.ANY)] * len(shapes),
        scratch_shapes=[
            pltpu.VMEM((steps, rows // steps) + shape[1:], kind),
            pltpu.SemaphoreType.DMA((steps + 1,)),
        ],
        cost_estimate=pl.CostEstimate(
            flops=2 * sum(left.size for left in lefts) * columns,
            bytes_accessed=4 * rows * columns,
            transcendentals=0,
        ),
        compiler_params=pltpu.CompilerParams(vmem_limit_bytes=16 << 20),
    )(*operands)


def work(mask, inputs, fwd_positions, weight, stash, key_grad, bwd_positions):
    width, heads, head_size = weight.shape
    rows = inputs.shape[0]

    replicas = lax.axis_size("dp")
    replica = lax.axis_index("dp")
    share = width // replicas
    square = lax.axis_size("section") == 4 and mask == 2
    crossed = lax.axis_size("section") == 4 and mask == 3
    cut = rows // 4 if square else rows
    held = [swapped(stash[:cut], "section", mask)]
    if square:
        held.append(swapped(stash[cut:], "section", mask))

    def block_of(owner):
        start = owner * share
        return jnp.concatenate(
            [lax.dynamic_slice_in_dim(piece, start, share, 1) for piece in held]
        )

    blocks = [block_of((replica + j) % replicas) for j in range(replicas)]
    flat_weight = weight.reshape(width, heads * head_size)

    back_cos, back_sin = rope_tables(bwd_positions, head_size)
    grad_pre = rotate(
        key_grad.astype(jnp.float32), back_cos[:, None], back_sin[:, None], -1.0
    ).astype(jnp.bfloat16)
    grad_flat = grad_pre.reshape(rows, heads * head_size)
    copies = jnp.broadcast_to(grad_flat, (replicas, *grad_flat.shape))
    grads_all = exchanged(after(copies, held[0]) if square else copies)
    grads_all = [
        lax.dynamic_index_in_dim(grads_all, (replica - j) % replicas, 0, keepdims=False)
        for j in range(replicas)
    ]

    input_grad = jnp.einsum(
        "rn,dn->rd", grad_flat, flat_weight, preferred_element_type=jnp.float32
    ).astype(jnp.bfloat16)
    if square:
        half = rows // 2
        upper, lower, ahead = after((input_grad[:half], input_grad[half:], inputs), held[0])
        odd = lax.axis_index("section") % 2 == 1
        upper = swapped(upper, "section", 1)
        lower_by_2 = lax.ppermute(lower, "section", [(0, 2), (2, 0)])
        evicted = swapped(ahead, "section", mask)
        upper_by_2 = lax.ppermute(after(upper, blocks), "section", [(1, 3), (3, 1)])
        lower = swapped(jnp.where(odd, lower, after(lower_by_2, blocks)), "section", 1)
        grad_in = [(upper, upper_by_2), lower]
        blocks[-1] = after(blocks[-1], (upper, blocks[1], blocks[2]))
    elif crossed:
        evicted = lax.ppermute(inputs, "section", [(0, 3), (2, 1), (3, 0)])
        grad_in = [shifted(input_grad, "section", -1)]
        evicted_2 = lax.ppermute(after(inputs, input_grad), "section", [(1, 2)])
    else:
        evicted = swapped(inputs, "section", mask)
        grad_in = [shifted(after(input_grad, blocks), "section", -1)]

    rows_all = [shifted(block, "dp", j) if j else block for j, block in enumerate(blocks)]

    products = jnp.dot(
        after(inputs, rows_all[1]),
        flat_weight,
        preferred_element_type=jnp.float32,
    )
    members = lax.axis_size("tensor")
    me = lax.axis_index("tensor")
    my_rows = rows // members
    summed = lax.dynamic_slice_in_dim(products, me * my_rows, my_rows, 0)
    for j in range(1, members):
        other = lax.dynamic_slice_in_dim(products, (me + j) % members * my_rows, my_rows, 0)
        summed = summed + shifted(other.astype(jnp.bfloat16), "tensor", j).astype(jnp.float32)
    my_positions = lax.dynamic_slice_in_dim(fwd_positions, me * my_rows, my_rows, 0)
    cosine, sine = rope_tables(my_positions, head_size)
    key_out = rotate(
        summed.reshape(my_rows, heads, head_size), cosine[:, None], sine[:, None], 1.0
    ).astype(jnp.bfloat16)

    lefts = [jnp.concatenate(rows_all[:-1], 0), rows_all[-1]]
    rights = [jnp.concatenate(grads_all[:-1], 0), grads_all[-1]]
    if square:
        (weight_grad,) = summed_products(lefts, rights, heads)
        grad_in, evicted = after((grad_in, evicted), weight_grad)
        key_out, grad_in, evicted = stored([key_out], grad_in, [evicted])
    else:
        weight_grad, evicted = summed_products(lefts, rights, heads, evicted)
        if crossed:
            key_out, grad_in, evicted = stored(
                [key_out], grad_in, [evicted_2], patched=2, into=evicted
            )
        else:
            key_out, grad_in = stored([key_out], grad_in)
    return key_out, grad_in, evicted, weight_grad


def body(fwd_input, fwd_positions, key_weight, stash, partner, key_grad, bwd_positions):
    sections = lax.axis_size("section")
    first = sections // 2
    branches = [
        lambda *blocks, mask=mask: work(mask, *blocks) for mask in range(first, sections)
    ]
    key_out, grad_in, evicted, weight_grad = lax.switch(
        partner[0] - first,
        branches,
        fwd_input[0, 0],
        fwd_positions[0, 0],
        key_weight[0],
        stash[0, 0],
        key_grad[0, 0],
        bwd_positions[0, 0],
    )
    return key_out[None, None], grad_in[None, None], evicted[None, None], weight_grad[None]


def solution(mesh):
    placed = (
        P("dp", "section", None, "tensor"),
        P("dp", "section", None),
        P("section", "tensor", None, None),
        P("dp", "section", None, "tensor"),
        P(),
        P("dp", "section", None, None, None),
        P("dp", "section", None),
    )
    return jax.shard_map(
        body,
        mesh=mesh,
        in_specs=placed,
        out_specs=(
            P("dp", "section", "tensor", None, None),
            P("dp", "section", None, "tensor"),
            P("dp", "section", None, "tensor"),
            P("section", ("tensor", "dp"), None, None),
        ),
        check_vma=False,
    )
```

```python
import functools

import jax
import jax.numpy as jnp
from jax import lax
from jax.experimental import pallas as pl
from jax.experimental.pallas import tpu as pltpu
from jax.sharding import PartitionSpec as P

THETA = 500000.0


def shifted(value, axis, distance):
    size = lax.axis_size(axis)
    return lax.ppermute(value, axis, [(i, (i + distance) % size) for i in range(size)])


def swapped(value, axis, mask):
    size = lax.axis_size(axis)
    return lax.ppermute(value, axis, [(i, i ^ mask) for i in range(size)])


def exchanged(blocks, groups=None):
    return lax.all_to_all(blocks, "dp", 0, 0, axis_index_groups=groups, tiled=True)


def after(value, earlier):
    return lax.optimization_barrier((value, earlier))[0]


def rope_tables(positions, head_size):
    half = head_size // 2
    freqs = THETA ** (-(2.0 * jnp.arange(half, dtype=jnp.float32)) / head_size)
    angles = positions.astype(jnp.float32)[..., None] * freqs
    return (jnp.cos(angles), jnp.sin(angles))


def rotate(keys, cosine, sine, sign):
    half = keys.shape[-1] // 2
    first = keys[..., :half]
    second = keys[..., half:]
    return jnp.concatenate(
        [first * cosine - sign * second * sine, second * cosine + sign * first * sine], axis=-1
    )


def store_kernel(places, patched, *refs):
    outs = max(out for out, _ in places) + 1
    parts, outs, sems = refs[: len(places)], refs[-1 - outs : -1], refs[-1]
    copies = [
        pltpu.make_async_copy(part, outs[out].at[pl.ds(row, part.shape[0])], sems.at[i])
        for i, (part, (out, row)) in enumerate(zip(parts, places))
    ]
    always = copies if patched is None else copies[:-1]
    for copy in always:
        copy.start()
    if patched is not None:
        here = lax.axis_index("section") == patched
        pl.when(here)(copies[-1].start)
        pl.when(here)(copies[-1].wait)
    for copy in always:
        copy.wait()


def stored(*groups, patched=None, into=None):
    places, shapes = [], []
    for out, group in enumerate(groups):
        row = 0
        for part in group:
            places.append((out, row))
            row += part.shape[0]
        shapes.append(pltpu.HBM((row,) + part.shape[1:], part.dtype))
    operands = [pltpu.with_memory_space_constraint(part, pltpu.VMEM) for part in sum(groups, [])]
    size = sum(part.size * part.dtype.itemsize for part in operands)
    aliases = {}
    if patched is not None:
        aliases = {len(operands): len(groups) - 1}
        operands.append(pltpu.with_memory_space_constraint(into, pltpu.HBM))
    return pl.pallas_call(
        functools.partial(store_kernel, tuple(places), patched),
        out_shape=shapes,
        in_specs=[pl.BlockSpec(memory_space=pl.ANY)] * len(operands),
        out_specs=[pl.BlockSpec(memory_space=pl.ANY)] * len(groups),
        scratch_shapes=[pltpu.SemaphoreType.DMA((len(places),))],
        input_output_aliases=aliases,
        cost_estimate=pl.CostEstimate(flops=0, bytes_accessed=2 * size, transcendentals=0),
        compiler_params=pltpu.CompilerParams(vmem_limit_bytes=1 << 20),
    )(*operands)


def product_kernel(count, *refs):
    lefts, rights, refs = refs[:count], refs[count : 2 * count], refs[2 * count :]
    copies = []
    if len(refs) == 3:
        out, buffer, sems = refs
    else:
        array, out, array_out, buffer, sems = refs
        copies.append(pltpu.make_async_copy(array, array_out, sems.at[buffer.shape[0]]))
        copies[0].start()
    steps, step, heads, _ = buffer.shape
    for i in range(steps):
        total = sum(
            lax.dot_general(
                left[:, i * step : (i + 1) * step],
                right[...],
                (((0,), (0,)), ((), ())),
                preferred_element_type=jnp.float32,
            )
            for left, right in zip(lefts, rights)
        )
        buffer[i] = pltpu.einshape("a(bc)->abc", total, b=heads).astype(out.dtype)
        copies.append(
            pltpu.make_async_copy(buffer.at[i], out.at[pl.ds(i * step, step)], sems.at[i])
        )
        copies[-1].start()
    for copy in copies:
        copy.wait()


def summed_products(lefts, rights, heads, array=None):
    rows, columns = lefts[0].shape[1], rights[0].shape[1]
    steps = 4 if rows % 1024 == 0 else 1
    kind = lefts[0].dtype
    shape = (rows, heads, columns // heads)
    shapes, operands = [pltpu.HBM(shape, kind)], [*lefts, *rights]
    specs = [pl.BlockSpec(memory_space=pltpu.VMEM)] * len(operands)
    if array is not None:
        shapes.append(pltpu.HBM(array.shape, array.dtype))
        operands.append(pltpu.with_memory_space_constraint(array, pltpu.VMEM))
        specs.append(pl.BlockSpec(memory_space=pl.ANY))
    return pl.pallas_call(
        functools.partial(product_kernel, len(lefts)),
        out_shape=shapes,
        in_specs=specs,
        out_specs=[pl.BlockSpec(memory_space=pl.ANY)] * len(shapes),
        scratch_shapes=[
            pltpu.VMEM((steps, rows // steps) + shape[1:], kind),
            pltpu.SemaphoreType.DMA((steps + 1,)),
        ],
        cost_estimate=pl.CostEstimate(
            flops=2 * sum(left.size for left in lefts) * columns,
            bytes_accessed=4 * rows * columns,
            transcendentals=0,
        ),
        compiler_params=pltpu.CompilerParams(vmem_limit_bytes=16 << 20),
    )(*operands)


def sent(blocks):
    return [shifted(block, "dp", j) if j else block for j, block in enumerate(blocks)]


def work(mask, inputs, fwd_positions, weight, stash, key_grad, bwd_positions):
    width, heads, head_size = weight.shape
    rows = inputs.shape[0]

    replicas = lax.axis_size("dp")
    replica = lax.axis_index("dp")
    share = width // replicas
    square = lax.axis_size("section") == 4 and mask == 2
    crossed = lax.axis_size("section") == 4 and mask == 3
    cut = rows // 4 if square else rows
    held = [swapped(stash[:cut], "section", mask)]
    if square:
        held.append(swapped(stash[cut:], "section", mask))

    def block_of(owner):
        start = owner * share
        return jnp.concatenate(
            [lax.dynamic_slice_in_dim(piece, start, share, 1) for piece in held]
        )

    blocks = [block_of((replica + j) % replicas) for j in range(replicas)]
    flat_weight = weight.reshape(width, heads * head_size)

    back_cos, back_sin = rope_tables(bwd_positions, head_size)
    grad_pre = rotate(
        key_grad.astype(jnp.float32), back_cos[:, None], back_sin[:, None], -1.0
    ).astype(jnp.bfloat16)
    grad_flat = grad_pre.reshape(rows, heads * head_size)
    copies = jnp.broadcast_to(grad_flat, (replicas, *grad_flat.shape))
    grads_all = exchanged(after(copies, held[0]) if square else copies)
    grads_all = [
        lax.dynamic_index_in_dim(grads_all, (replica - j) % replicas, 0, keepdims=False)
        for j in range(replicas)
    ]

    input_grad = jnp.einsum(
        "rn,dn->rd", grad_flat, flat_weight, preferred_element_type=jnp.float32
    ).astype(jnp.bfloat16)
    if square:
        half = rows // 2
        upper, lower, ahead = after((input_grad[:half], input_grad[half:], inputs), held[0])
        upper = swapped(upper, "section", 1)
        lower = lax.ppermute(lower, "section", [(0, 2), (1, 1), (2, 0), (3, 3)])
        evicted = swapped(ahead, "section", mask)
        blocks[-1] = after(blocks[-1], upper)
        rows_all = sent(blocks)
        upper = lax.ppermute(after(upper, blocks), "section", [(0, 0), (1, 3), (2, 2), (3, 1)])
        lower = swapped(after(lower, rows_all[1]), "section", 1)
        grad_in = [upper, lower]
    elif crossed:
        evicted = lax.ppermute(inputs, "section", [(0, 3), (2, 1), (3, 0)])
        grad_in = [shifted(input_grad, "section", -1)]
        evicted_2 = lax.ppermute(after(inputs, input_grad), "section", [(1, 2)])
    else:
        evicted = swapped(inputs, "section", mask)
        grad_in = [shifted(after(input_grad, blocks), "section", -1)]

    if not square:
        rows_all = sent(blocks)

    products = jnp.dot(
        after(inputs, rows_all[1]),
        flat_weight,
        preferred_element_type=jnp.float32,
    )
    members = lax.axis_size("tensor")
    me = lax.axis_index("tensor")
    my_rows = rows // members
    summed = lax.dynamic_slice_in_dim(products, me * my_rows, my_rows, 0)
    for j in range(1, members):
        other = lax.dynamic_slice_in_dim(products, (me + j) % members * my_rows, my_rows, 0)
        summed = summed + shifted(other.astype(jnp.bfloat16), "tensor", j).astype(jnp.float32)
    my_positions = lax.dynamic_slice_in_dim(fwd_positions, me * my_rows, my_rows, 0)
    cosine, sine = rope_tables(my_positions, head_size)
    key_out = rotate(
        summed.reshape(my_rows, heads, head_size), cosine[:, None], sine[:, None], 1.0
    ).astype(jnp.bfloat16)

    lefts = [jnp.concatenate(rows_all[:-1], 0), rows_all[-1]]
    rights = [jnp.concatenate(grads_all[:-1], 0), grads_all[-1]]
    if square:
        (weight_grad,) = summed_products(lefts, rights, heads)
        grad_in, evicted = after((grad_in, evicted), weight_grad)
        key_out, grad_in, evicted = stored([key_out], grad_in, [evicted])
    else:
        weight_grad, evicted = summed_products(lefts, rights, heads, evicted)
        if crossed:
            key_out, grad_in, evicted = stored(
                [key_out], grad_in, [evicted_2], patched=2, into=evicted
            )
        else:
            key_out, grad_in = stored([key_out], grad_in)
    return key_out, grad_in, evicted, weight_grad


def body(fwd_input, fwd_positions, key_weight, stash, partner, key_grad, bwd_positions):
    sections = lax.axis_size("section")
    first = sections // 2
    branches = [
        lambda *blocks, mask=mask: work(mask, *blocks) for mask in range(first, sections)
    ]
    key_out, grad_in, evicted, weight_grad = lax.switch(
        partner[0] - first,
        branches,
        fwd_input[0, 0],
        fwd_positions[0, 0],
        key_weight[0],
        stash[0, 0],
        key_grad[0, 0],
        bwd_positions[0, 0],
    )
    return key_out[None, None], grad_in[None, None], evicted[None, None], weight_grad[None]


def solution(mesh):
    placed = (
        P("dp", "section", None, "tensor"),
        P("dp", "section", None),
        P("section", "tensor", None, None),
        P("dp", "section", None, "tensor"),
        P(),
        P("dp", "section", None, None, None),
        P("dp", "section", None),
    )
    return jax.shard_map(
        body,
        mesh=mesh,
        in_specs=placed,
        out_specs=(
            P("dp", "section", "tensor", None, None),
            P("dp", "section", None, "tensor"),
            P("dp", "section", None, "tensor"),
            P("section", ("tensor", "dp"), None, None),
        ),
        check_vma=False,
    )
```

```python
import functools

import jax
import jax.numpy as jnp
from jax import lax
from jax.experimental import pallas as pl
from jax.experimental.pallas import tpu as pltpu
from jax.sharding import PartitionSpec as P

THETA = 500000.0


def shifted(value, axis, distance):
    size = lax.axis_size(axis)
    return lax.ppermute(value, axis, [(i, (i + distance) % size) for i in range(size)])


def swapped(value, axis, mask):
    size = lax.axis_size(axis)
    return lax.ppermute(value, axis, [(i, i ^ mask) for i in range(size)])


def exchanged(blocks, groups=None):
    return lax.all_to_all(blocks, "dp", 0, 0, axis_index_groups=groups, tiled=True)


def after(value, earlier):
    return lax.optimization_barrier((value, earlier))[0]


def rope_tables(positions, head_size):
    half = head_size // 2
    freqs = THETA ** (-(2.0 * jnp.arange(half, dtype=jnp.float32)) / head_size)
    angles = positions.astype(jnp.float32)[..., None] * freqs
    return (jnp.cos(angles), jnp.sin(angles))


def rotate(keys, cosine, sine, sign):
    half = keys.shape[-1] // 2
    first = keys[..., :half]
    second = keys[..., half:]
    return jnp.concatenate(
        [first * cosine - sign * second * sine, second * cosine + sign * first * sine], axis=-1
    )


def store_kernel(places, *refs):
    outs = max(out for out, _, _ in places) + 1
    parts, outs, sems = refs[: -1 - outs], refs[-1 - outs : -1], refs[-1]
    parts = list(parts)
    copies = []
    for i, (out, row, choice) in enumerate(places):
        part = parts.pop(0)
        rows = outs[out].at[pl.ds(row, part.shape[0])]
        copies.append(pltpu.make_async_copy(part, rows, sems.at[i]))
        if choice:
            other = pltpu.make_async_copy(parts.pop(0), rows, sems.at[i])
            odd = lax.axis_index("section") % 2 == 1
            pl.when(odd)(other.start)
            pl.when(jnp.logical_not(odd))(copies[i].start)
        else:
            copies[i].start()
    for copy in copies:
        copy.wait()


def stored(*groups):
    places, shapes, parts = [], [], []
    for out, group in enumerate(groups):
        row = 0
        for part in group:
            choice = isinstance(part, tuple)
            parts.extend(part if choice else [part])
            places.append((out, row, choice))
            row += parts[-1].shape[0]
        shapes.append(pltpu.HBM((row,) + parts[-1].shape[1:], parts[-1].dtype))
    parts = [pltpu.with_memory_space_constraint(part, pltpu.VMEM) for part in parts]
    size = sum(part.size * part.dtype.itemsize for part in parts)
    return pl.pallas_call(
        functools.partial(store_kernel, tuple(places)),
        out_shape=shapes,
        in_specs=[pl.BlockSpec(memory_space=pl.ANY)] * len(parts),
        out_specs=[pl.BlockSpec(memory_space=pl.ANY)] * len(groups),
        scratch_shapes=[pltpu.SemaphoreType.DMA((len(places),))],
        cost_estimate=pl.CostEstimate(flops=0, bytes_accessed=2 * size, transcendentals=0),
        compiler_params=pltpu.CompilerParams(vmem_limit_bytes=1 << 20),
    )(*parts)


def patch_kernel(section, key_part, part, patch, _, key_out, out, patched, sems):
    copies = [
        pltpu.make_async_copy(source, target, sems.at[i])
        for i, (source, target) in enumerate([(key_part, key_out), (part, out), (patch, patched)])
    ]
    here = lax.axis_index("section") == section
    copies[0].start()
    copies[1].start()
    pl.when(here)(copies[2].start)
    pl.when(here)(copies[2].wait)
    copies[0].wait()
    copies[1].wait()


def stored_and_patched(keys, part, patch, section, into):
    parts = [pltpu.with_memory_space_constraint(x, pltpu.VMEM) for x in (keys, part, patch)]
    size = sum(x.size * x.dtype.itemsize for x in parts)
    return pl.pallas_call(
        functools.partial(patch_kernel, section),
        out_shape=[pltpu.HBM(x.shape, x.dtype) for x in parts],
        in_specs=[pl.BlockSpec(memory_space=pl.ANY)] * 4,
        out_specs=[pl.BlockSpec(memory_space=pl.ANY)] * 3,
        scratch_shapes=[pltpu.SemaphoreType.DMA((3,))],
        input_output_aliases={3: 2},
        cost_estimate=pl.CostEstimate(flops=0, bytes_accessed=2 * size, transcendentals=0),
        compiler_params=pltpu.CompilerParams(vmem_limit_bytes=1 << 20),
    )(*parts, pltpu.with_memory_space_constraint(into, pltpu.HBM))


def product_kernel(count, *refs):
    lefts, rights, refs = refs[:count], refs[count : 2 * count], refs[2 * count :]
    copies = []
    if len(refs) == 3:
        out, buffer, sems = refs
    else:
        array, out, array_out, buffer, sems = refs
        copies.append(pltpu.make_async_copy(array, array_out, sems.at[buffer.shape[0]]))
        copies[0].start()
    steps, step, heads, _ = buffer.shape
    for i in range(steps):
        total = sum(
            lax.dot_general(
                left[:, i * step : (i + 1) * step],
                right[...],
                (((0,), (0,)), ((), ())),
                preferred_element_type=jnp.float32,
            )
            for left, right in zip(lefts, rights)
        )
        buffer[i] = pltpu.einshape("a(bc)->abc", total, b=heads).astype(out.dtype)
        copies.append(
            pltpu.make_async_copy(buffer.at[i], out.at[pl.ds(i * step, step)], sems.at[i])
        )
        copies[-1].start()
    for copy in copies:
        copy.wait()


def summed_products(lefts, rights, heads, array=None):
    rows, columns = lefts[0].shape[1], rights[0].shape[1]
    steps = 4 if rows % 1024 == 0 else 1
    kind = lefts[0].dtype
    shape = (rows, heads, columns // heads)
    shapes, operands = [pltpu.HBM(shape, kind)], [*lefts, *rights]
    specs = [pl.BlockSpec(memory_space=pltpu.VMEM)] * len(operands)
    if array is not None:
        shapes.append(pltpu.HBM(array.shape, array.dtype))
        operands.append(pltpu.with_memory_space_constraint(array, pltpu.VMEM))
        specs.append(pl.BlockSpec(memory_space=pl.ANY))
    return pl.pallas_call(
        functools.partial(product_kernel, len(lefts)),
        out_shape=shapes,
        in_specs=specs,
        out_specs=[pl.BlockSpec(memory_space=pl.ANY)] * len(shapes),
        scratch_shapes=[
            pltpu.VMEM((steps, rows // steps) + shape[1:], kind),
            pltpu.SemaphoreType.DMA((steps + 1,)),
        ],
        cost_estimate=pl.CostEstimate(
            flops=2 * sum(left.size for left in lefts) * columns,
            bytes_accessed=4 * rows * columns,
            transcendentals=0,
        ),
        compiler_params=pltpu.CompilerParams(vmem_limit_bytes=16 << 20),
    )(*operands)


def sent(blocks):
    return [shifted(block, "dp", j) if j else block for j, block in enumerate(blocks)]


def work(mask, inputs, fwd_positions, weight, stash, key_grad, bwd_positions):
    width, heads, head_size = weight.shape
    rows = inputs.shape[0]

    replicas = lax.axis_size("dp")
    replica = lax.axis_index("dp")
    share = width // replicas
    square = lax.axis_size("section") == 4 and mask == 2
    crossed = lax.axis_size("section") == 4 and mask == 3
    cut = rows // 4 if square else rows
    held = [swapped(stash[:cut], "section", mask)]
    if square:
        held.append(swapped(stash[cut:], "section", mask))

    def block_of(owner):
        start = owner * share
        return jnp.concatenate(
            [lax.dynamic_slice_in_dim(piece, start, share, 1) for piece in held]
        )

    blocks = [block_of((replica + j) % replicas) for j in range(replicas)]
    flat_weight = weight.reshape(width, heads * head_size)

    back_cos, back_sin = rope_tables(bwd_positions, head_size)
    grad_pre = rotate(
        key_grad.astype(jnp.float32), back_cos[:, None], back_sin[:, None], -1.0
    ).astype(jnp.bfloat16)
    grad_flat = grad_pre.reshape(rows, heads * head_size)
    copies = jnp.broadcast_to(grad_flat, (replicas, *grad_flat.shape))
    grads_all = exchanged(after(copies, held[0]) if square else copies)
    grads_all = [
        lax.dynamic_index_in_dim(grads_all, (replica - j) % replicas, 0, keepdims=False)
        for j in range(replicas)
    ]

    input_grad = jnp.einsum(
        "rn,dn->rd", grad_flat, flat_weight, preferred_element_type=jnp.float32
    ).astype(jnp.bfloat16)
    if square:
        half = rows // 2
        upper, lower, ahead = after((input_grad[:half], input_grad[half:], inputs), held[0])
        odd = lax.axis_index("section") % 2 == 1
        upper = swapped(upper, "section", 1)
        lower_by_2 = lax.ppermute(lower, "section", [(0, 2), (2, 0)])
        evicted = swapped(ahead, "section", mask)
        blocks[-1] = after(blocks[-1], upper)
        rows_all = sent(blocks)
        upper_by_2 = lax.ppermute(after(upper, blocks), "section", [(1, 3), (3, 1)])
        lower = swapped(jnp.where(odd, lower, after(lower_by_2, rows_all[1])), "section", 1)
        grad_in = [(upper, upper_by_2), lower]
    elif crossed:
        evicted = lax.ppermute(inputs, "section", [(0, 3), (2, 1), (3, 0)])
        grad_in = [shifted(input_grad, "section", -1)]
        evicted_2 = lax.ppermute(after(inputs, input_grad), "section", [(1, 2)])
    else:
        evicted = swapped(inputs, "section", mask)
        grad_in = [shifted(after(input_grad, blocks), "section", -1)]

    if not square:
        rows_all = sent(blocks)

    products = jnp.dot(
        after(inputs, rows_all[1]),
        flat_weight,
        preferred_element_type=jnp.float32,
    )
    members = lax.axis_size("tensor")
    me = lax.axis_index("tensor")
    my_rows = rows // members
    summed = lax.dynamic_slice_in_dim(products, me * my_rows, my_rows, 0)
    for j in range(1, members):
        other = lax.dynamic_slice_in_dim(products, (me + j) % members * my_rows, my_rows, 0)
        summed = summed + shifted(other.astype(jnp.bfloat16), "tensor", j).astype(jnp.float32)
    my_positions = lax.dynamic_slice_in_dim(fwd_positions, me * my_rows, my_rows, 0)
    cosine, sine = rope_tables(my_positions, head_size)
    key_out = rotate(
        summed.reshape(my_rows, heads, head_size), cosine[:, None], sine[:, None], 1.0
    ).astype(jnp.bfloat16)

    lefts = [jnp.concatenate(rows_all[:-1], 0), rows_all[-1]]
    rights = [jnp.concatenate(grads_all[:-1], 0), grads_all[-1]]
    if square:
        (weight_grad,) = summed_products(lefts, rights, heads)
        grad_in, evicted = after((grad_in, evicted), weight_grad)
        key_out, grad_in, evicted = stored([key_out], grad_in, [evicted])
    else:
        weight_grad, evicted = summed_products(lefts, rights, heads, evicted)
        if crossed:
            key_out, grad_in, evicted = stored_and_patched(
                key_out, grad_in[0], evicted_2, 2, evicted
            )
        else:
            key_out, grad_in = stored([key_out], grad_in)
    return key_out, grad_in, evicted, weight_grad


def body(fwd_input, fwd_positions, key_weight, stash, partner, key_grad, bwd_positions):
    sections = lax.axis_size("section")
    first = sections // 2
    branches = [
        lambda *blocks, mask=mask: work(mask, *blocks) for mask in range(first, sections)
    ]
    key_out, grad_in, evicted, weight_grad = lax.switch(
        partner[0] - first,
        branches,
        fwd_input[0, 0],
        fwd_positions[0, 0],
        key_weight[0],
        stash[0, 0],
        key_grad[0, 0],
        bwd_positions[0, 0],
    )
    return key_out[None, None], grad_in[None, None], evicted[None, None], weight_grad[None]


def solution(mesh):
    placed = (
        P("dp", "section", None, "tensor"),
        P("dp", "section", None),
        P("section", "tensor", None, None),
        P("dp", "section", None, "tensor"),
        P(),
        P("dp", "section", None, None, None),
        P("dp", "section", None),
    )
    return jax.shard_map(
        body,
        mesh=mesh,
        in_specs=placed,
        out_specs=(
            P("dp", "section", "tensor", None, None),
            P("dp", "section", None, "tensor"),
            P("dp", "section", None, "tensor"),
            P("section", ("tensor", "dp"), None, None),
        ),
        check_vma=False,
    )
```

```python
import functools

import jax
import jax.numpy as jnp
from jax import lax
from jax.experimental import pallas as pl
from jax.experimental.pallas import tpu as pltpu
from jax.sharding import PartitionSpec as P

THETA = 500000.0


def shifted(value, axis, distance):
    size = lax.axis_size(axis)
    return lax.ppermute(value, axis, [(i, (i + distance) % size) for i in range(size)])


def swapped(value, axis, mask):
    size = lax.axis_size(axis)
    return lax.ppermute(value, axis, [(i, i ^ mask) for i in range(size)])


def exchanged(blocks, groups=None):
    return lax.all_to_all(blocks, "dp", 0, 0, axis_index_groups=groups, tiled=True)


def after(value, earlier):
    return lax.optimization_barrier((value, earlier))[0]


def rope_tables(positions, head_size):
    half = head_size // 2
    freqs = THETA ** (-(2.0 * jnp.arange(half, dtype=jnp.float32)) / head_size)
    angles = positions.astype(jnp.float32)[..., None] * freqs
    return (jnp.cos(angles), jnp.sin(angles))


def rotate(keys, cosine, sine, sign):
    half = keys.shape[-1] // 2
    first = keys[..., :half]
    second = keys[..., half:]
    return jnp.concatenate(
        [first * cosine - sign * second * sine, second * cosine + sign * first * sine], axis=-1
    )


def store_kernel(places, *refs):
    outs = max(out for out, _, _ in places) + 1
    parts, outs, sems = refs[: -1 - outs], refs[-1 - outs : -1], refs[-1]
    parts = list(parts)
    copies = []
    for i, (out, row, choice) in enumerate(places):
        part = parts.pop(0)
        rows = outs[out].at[pl.ds(row, part.shape[0])]
        copies.append(pltpu.make_async_copy(part, rows, sems.at[i]))
        if choice:
            other = pltpu.make_async_copy(parts.pop(0), rows, sems.at[i])
            odd = lax.axis_index("section") % 2 == 1
            pl.when(odd)(other.start)
            pl.when(jnp.logical_not(odd))(copies[i].start)
        else:
            copies[i].start()
    for copy in copies:
        copy.wait()


def stored(*groups):
    places, shapes, parts = [], [], []
    for out, group in enumerate(groups):
        row = 0
        for part in group:
            choice = isinstance(part, tuple)
            parts.extend(part if choice else [part])
            places.append((out, row, choice))
            row += parts[-1].shape[0]
        shapes.append(pltpu.HBM((row,) + parts[-1].shape[1:], parts[-1].dtype))
    parts = [pltpu.with_memory_space_constraint(part, pltpu.VMEM) for part in parts]
    size = sum(part.size * part.dtype.itemsize for part in parts)
    return pl.pallas_call(
        functools.partial(store_kernel, tuple(places)),
        out_shape=shapes,
        in_specs=[pl.BlockSpec(memory_space=pl.ANY)] * len(parts),
        out_specs=[pl.BlockSpec(memory_space=pl.ANY)] * len(groups),
        scratch_shapes=[pltpu.SemaphoreType.DMA((len(places),))],
        cost_estimate=pl.CostEstimate(flops=0, bytes_accessed=2 * size, transcendentals=0),
        compiler_params=pltpu.CompilerParams(vmem_limit_bytes=1 << 20),
    )(*parts)


def patch_kernel(section, key_part, part, patch, _, key_out, out, patched, sems):
    copies = [
        pltpu.make_async_copy(source, target, sems.at[i])
        for i, (source, target) in enumerate([(key_part, key_out), (part, out), (patch, patched)])
    ]
    here = lax.axis_index("section") == section
    copies[0].start()
    copies[1].start()
    pl.when(here)(copies[2].start)
    pl.when(here)(copies[2].wait)
    copies[0].wait()
    copies[1].wait()


def stored_and_patched(keys, part, patch, section, into):
    parts = [pltpu.with_memory_space_constraint(x, pltpu.VMEM) for x in (keys, part, patch)]
    size = sum(x.size * x.dtype.itemsize for x in parts)
    return pl.pallas_call(
        functools.partial(patch_kernel, section),
        out_shape=[pltpu.HBM(x.shape, x.dtype) for x in parts],
        in_specs=[pl.BlockSpec(memory_space=pl.ANY)] * 4,
        out_specs=[pl.BlockSpec(memory_space=pl.ANY)] * 3,
        scratch_shapes=[pltpu.SemaphoreType.DMA((3,))],
        input_output_aliases={3: 2},
        cost_estimate=pl.CostEstimate(flops=0, bytes_accessed=2 * size, transcendentals=0),
        compiler_params=pltpu.CompilerParams(vmem_limit_bytes=1 << 20),
    )(*parts, pltpu.with_memory_space_constraint(into, pltpu.HBM))


def product_kernel(count, *refs):
    lefts, rights, refs = refs[:count], refs[count : 2 * count], refs[2 * count :]
    copies = []
    if len(refs) == 3:
        out, buffer, sems = refs
    else:
        array, out, array_out, buffer, sems = refs
        copies.append(pltpu.make_async_copy(array, array_out, sems.at[buffer.shape[0]]))
        copies[0].start()
    steps, step, heads, _ = buffer.shape
    for i in range(steps):
        total = sum(
            lax.dot_general(
                left[:, i * step : (i + 1) * step],
                right[...],
                (((0,), (0,)), ((), ())),
                preferred_element_type=jnp.float32,
            )
            for left, right in zip(lefts, rights)
        )
        buffer[i] = pltpu.einshape("a(bc)->abc", total, b=heads).astype(out.dtype)
        copies.append(
            pltpu.make_async_copy(buffer.at[i], out.at[pl.ds(i * step, step)], sems.at[i])
        )
        copies[-1].start()
    for copy in copies:
        copy.wait()


def summed_products(lefts, rights, heads, array=None):
    rows, columns = lefts[0].shape[1], rights[0].shape[1]
    steps = 4 if rows % 1024 == 0 else 1
    kind = lefts[0].dtype
    shape = (rows, heads, columns // heads)
    shapes, operands = [pltpu.HBM(shape, kind)], [*lefts, *rights]
    specs = [pl.BlockSpec(memory_space=pltpu.VMEM)] * len(operands)
    if array is not None:
        shapes.append(pltpu.HBM(array.shape, array.dtype))
        operands.append(pltpu.with_memory_space_constraint(array, pltpu.VMEM))
        specs.append(pl.BlockSpec(memory_space=pl.ANY))
    return pl.pallas_call(
        functools.partial(product_kernel, len(lefts)),
        out_shape=shapes,
        in_specs=specs,
        out_specs=[pl.BlockSpec(memory_space=pl.ANY)] * len(shapes),
        scratch_shapes=[
            pltpu.VMEM((steps, rows // steps) + shape[1:], kind),
            pltpu.SemaphoreType.DMA((steps + 1,)),
        ],
        cost_estimate=pl.CostEstimate(
            flops=2 * sum(left.size for left in lefts) * columns,
            bytes_accessed=4 * rows * columns,
            transcendentals=0,
        ),
        compiler_params=pltpu.CompilerParams(vmem_limit_bytes=16 << 20),
    )(*operands)


def work(mask, inputs, fwd_positions, weight, stash, key_grad, bwd_positions):
    width, heads, head_size = weight.shape
    rows = inputs.shape[0]

    replicas = lax.axis_size("dp")
    replica = lax.axis_index("dp")
    share = width // replicas
    square = lax.axis_size("section") == 4 and mask == 2
    crossed = lax.axis_size("section") == 4 and mask == 3
    cut = rows // 4 if square else rows
    held = [swapped(stash[:cut], "section", mask)]
    if square:
        held.append(swapped(stash[cut:], "section", mask))

    def block_of(owner):
        start = owner * share
        return jnp.concatenate(
            [lax.dynamic_slice_in_dim(piece, start, share, 1) for piece in held]
        )

    blocks = [block_of((replica + j) % replicas) for j in range(replicas)]
    flat_weight = weight.reshape(width, heads * head_size)

    back_cos, back_sin = rope_tables(bwd_positions, head_size)
    grad_pre = rotate(
        key_grad.astype(jnp.float32), back_cos[:, None], back_sin[:, None], -1.0
    ).astype(jnp.bfloat16)
    grad_flat = grad_pre.reshape(rows, heads * head_size)
    copies = jnp.broadcast_to(grad_flat, (replicas, *grad_flat.shape))
    grads_all = exchanged(after(copies, held[0]) if square else copies)
    grads_all = [
        lax.dynamic_index_in_dim(grads_all, (replica - j) % replicas, 0, keepdims=False)
        for j in range(replicas)
    ]

    input_grad = jnp.einsum(
        "rn,dn->rd", grad_flat, flat_weight, preferred_element_type=jnp.float32
    ).astype(jnp.bfloat16)
    if square:
        half = rows // 2
        upper, lower, ahead = after((input_grad[:half], input_grad[half:], inputs), held[0])
        odd = lax.axis_index("section") % 2 == 1
        upper = swapped(upper, "section", 1)
        lower_by_2 = lax.ppermute(lower, "section", [(0, 2), (2, 0)])
        evicted = swapped(ahead, "section", mask)
        upper_by_2 = lax.ppermute(after(upper, blocks), "section", [(1, 3), (3, 1)])
        lower = swapped(jnp.where(odd, lower, after(lower_by_2, blocks)), "section", 1)
        grad_in = [(upper, upper_by_2), lower]
        blocks[-1] = after(blocks[-1], upper)
    elif crossed:
        evicted = lax.ppermute(inputs, "section", [(0, 3), (2, 1), (3, 0)])
        grad_in = [shifted(input_grad, "section", -1)]
        evicted_2 = lax.ppermute(after(inputs, input_grad), "section", [(1, 2)])
    else:
        evicted = swapped(inputs, "section", mask)
        grad_in = [shifted(after(input_grad, blocks), "section", -1)]

    rows_all = [shifted(block, "dp", j) if j else block for j, block in enumerate(blocks)]

    products = jnp.dot(
        after(inputs, rows_all[1]),
        flat_weight,
        preferred_element_type=jnp.float32,
    )
    members = lax.axis_size("tensor")
    me = lax.axis_index("tensor")
    my_rows = rows // members
    summed = lax.dynamic_slice_in_dim(products, me * my_rows, my_rows, 0)
    for j in range(1, members):
        other = lax.dynamic_slice_in_dim(products, (me + j) % members * my_rows, my_rows, 0)
        summed = summed + shifted(other.astype(jnp.bfloat16), "tensor", j).astype(jnp.float32)
    my_positions = lax.dynamic_slice_in_dim(fwd_positions, me * my_rows, my_rows, 0)
    cosine, sine = rope_tables(my_positions, head_size)
    key_out = rotate(
        summed.reshape(my_rows, heads, head_size), cosine[:, None], sine[:, None], 1.0
    ).astype(jnp.bfloat16)

    lefts = [jnp.concatenate(rows_all[:-1], 0), rows_all[-1]]
    rights = [jnp.concatenate(grads_all[:-1], 0), grads_all[-1]]
    if square:
        (weight_grad,) = summed_products(lefts, rights, heads)
        grad_in, evicted = after((grad_in, evicted), weight_grad)
        key_out, grad_in, evicted = stored([key_out], grad_in, [evicted])
    else:
        weight_grad, evicted = summed_products(lefts, rights, heads, evicted)
        if crossed:
            key_out, grad_in, evicted = stored_and_patched(
                key_out, grad_in[0], evicted_2, 2, evicted
            )
        else:
            key_out, grad_in = stored([key_out], grad_in)
    return key_out, grad_in, evicted, weight_grad


def body(fwd_input, fwd_positions, key_weight, stash, partner, key_grad, bwd_positions):
    sections = lax.axis_size("section")
    first = sections // 2
    branches = [
        lambda *blocks, mask=mask: work(mask, *blocks) for mask in range(first, sections)
    ]
    key_out, grad_in, evicted, weight_grad = lax.switch(
        partner[0] - first,
        branches,
        fwd_input[0, 0],
        fwd_positions[0, 0],
        key_weight[0],
        stash[0, 0],
        key_grad[0, 0],
        bwd_positions[0, 0],
    )
    return key_out[None, None], grad_in[None, None], evicted[None, None], weight_grad[None]


def solution(mesh):
    placed = (
        P("dp", "section", None, "tensor"),
        P("dp", "section", None),
        P("section", "tensor", None, None),
        P("dp", "section", None, "tensor"),
        P(),
        P("dp", "section", None, None, None),
        P("dp", "section", None),
    )
    return jax.shard_map(
        body,
        mesh=mesh,
        in_specs=placed,
        out_specs=(
            P("dp", "section", "tensor", None, None),
            P("dp", "section", None, "tensor"),
            P("dp", "section", None, "tensor"),
            P("section", ("tensor", "dp"), None, None),
        ),
        check_vma=False,
    )
```

```python
import functools

import jax
import jax.numpy as jnp
from jax import lax
from jax.experimental import pallas as pl
from jax.experimental.pallas import tpu as pltpu
from jax.sharding import PartitionSpec as P

THETA = 500000.0


def shifted(value, axis, distance):
    size = lax.axis_size(axis)
    return lax.ppermute(value, axis, [(i, (i + distance) % size) for i in range(size)])


def swapped(value, axis, mask):
    size = lax.axis_size(axis)
    return lax.ppermute(value, axis, [(i, i ^ mask) for i in range(size)])


def exchanged(blocks, groups=None):
    return lax.all_to_all(blocks, "dp", 0, 0, axis_index_groups=groups, tiled=True)


def after(value, earlier):
    return lax.optimization_barrier((value, earlier))[0]


def rope_tables(positions, head_size):
    half = head_size // 2
    freqs = THETA ** (-(2.0 * jnp.arange(half, dtype=jnp.float32)) / head_size)
    angles = positions.astype(jnp.float32)[..., None] * freqs
    return (jnp.cos(angles), jnp.sin(angles))


def rotate(keys, cosine, sine, sign):
    half = keys.shape[-1] // 2
    first = keys[..., :half]
    second = keys[..., half:]
    return jnp.concatenate(
        [first * cosine - sign * second * sine, second * cosine + sign * first * sine], axis=-1
    )


def store_kernel(places, *refs):
    outs = max(out for out, _, _ in places) + 1
    parts, outs, sems = refs[: -1 - outs], refs[-1 - outs : -1], refs[-1]
    parts = list(parts)
    copies = []
    for i, (out, row, choice) in enumerate(places):
        part = parts.pop(0)
        rows = outs[out].at[pl.ds(row, part.shape[0])]
        copies.append(pltpu.make_async_copy(part, rows, sems.at[i]))
        if choice:
            other = pltpu.make_async_copy(parts.pop(0), rows, sems.at[i])
            odd = lax.axis_index("section") % 2 == 1
            pl.when(odd)(other.start)
            pl.when(jnp.logical_not(odd))(copies[i].start)
        else:
            copies[i].start()
    for copy in copies:
        copy.wait()


def stored(*groups):
    places, shapes, parts = [], [], []
    for out, group in enumerate(groups):
        row = 0
        for part in group:
            choice = isinstance(part, tuple)
            parts.extend(part if choice else [part])
            places.append((out, row, choice))
            row += parts[-1].shape[0]
        shapes.append(pltpu.HBM((row,) + parts[-1].shape[1:], parts[-1].dtype))
    parts = [pltpu.with_memory_space_constraint(part, pltpu.VMEM) for part in parts]
    size = sum(part.size * part.dtype.itemsize for part in parts)
    return pl.pallas_call(
        functools.partial(store_kernel, tuple(places)),
        out_shape=shapes,
        in_specs=[pl.BlockSpec(memory_space=pl.ANY)] * len(parts),
        out_specs=[pl.BlockSpec(memory_space=pl.ANY)] * len(groups),
        scratch_shapes=[pltpu.SemaphoreType.DMA((len(places),))],
        cost_estimate=pl.CostEstimate(flops=0, bytes_accessed=2 * size, transcendentals=0),
        compiler_params=pltpu.CompilerParams(vmem_limit_bytes=1 << 20),
    )(*parts)


def finish_kernel(key_part, part, _, key_out, out, sems):
    rows = out.at[pl.ds(out.shape[0] - part.shape[0], part.shape[0])]
    copies = [
        pltpu.make_async_copy(key_part, key_out, sems.at[0]),
        pltpu.make_async_copy(part, rows, sems.at[1]),
    ]
    for copy in copies:
        copy.start()
    for copy in copies:
        copy.wait()


def finished(keys, part, into):
    parts = [pltpu.with_memory_space_constraint(x, pltpu.VMEM) for x in (keys, part)]
    size = sum(x.size * x.dtype.itemsize for x in parts)
    return pl.pallas_call(
        finish_kernel,
        out_shape=[pltpu.HBM(x.shape, x.dtype) for x in (keys, into)],
        in_specs=[pl.BlockSpec(memory_space=pl.ANY)] * 3,
        out_specs=[pl.BlockSpec(memory_space=pl.ANY)] * 2,
        scratch_shapes=[pltpu.SemaphoreType.DMA((2,))],
        input_output_aliases={2: 1},
        cost_estimate=pl.CostEstimate(flops=0, bytes_accessed=2 * size, transcendentals=0),
        compiler_params=pltpu.CompilerParams(vmem_limit_bytes=1 << 20),
    )(*parts, pltpu.with_memory_space_constraint(into, pltpu.HBM))


def begin_kernel(part, out, sem):
    copy = pltpu.make_async_copy(part, out.at[pl.ds(0, part.shape[0])], sem)
    copy.start()
    copy.wait()


def begun(part, rows):
    return pl.pallas_call(
        begin_kernel,
        out_shape=pltpu.HBM((rows,) + part.shape[1:], part.dtype),
        in_specs=[pl.BlockSpec(memory_space=pl.ANY)],
        out_specs=pl.BlockSpec(memory_space=pl.ANY),
        scratch_shapes=[pltpu.SemaphoreType.DMA],
        cost_estimate=pl.CostEstimate(
            flops=0, bytes_accessed=2 * part.size * part.dtype.itemsize, transcendentals=0
        ),
        compiler_params=pltpu.CompilerParams(vmem_limit_bytes=1 << 20),
    )(pltpu.with_memory_space_constraint(part, pltpu.VMEM))


def product_kernel(count, *refs):
    lefts, rights, refs = refs[:count], refs[count : 2 * count], refs[2 * count :]
    copies = []
    if len(refs) == 3:
        out, buffer, sems = refs
    else:
        array, out, array_out, buffer, sems = refs
        copies.append(pltpu.make_async_copy(array, array_out, sems.at[buffer.shape[0]]))
        copies[0].start()
    steps, step, heads, _ = buffer.shape
    for i in range(steps):
        total = sum(
            lax.dot_general(
                left[:, i * step : (i + 1) * step],
                right[...],
                (((0,), (0,)), ((), ())),
                preferred_element_type=jnp.float32,
            )
            for left, right in zip(lefts, rights)
        )
        buffer[i] = pltpu.einshape("a(bc)->abc", total, b=heads).astype(out.dtype)
        copies.append(
            pltpu.make_async_copy(buffer.at[i], out.at[pl.ds(i * step, step)], sems.at[i])
        )
        copies[-1].start()
    for copy in copies:
        copy.wait()


def summed_products(lefts, rights, heads, array=None):
    rows, columns = lefts[0].shape[1], rights[0].shape[1]
    steps = 4 if rows % 1024 == 0 else 1
    kind = lefts[0].dtype
    shape = (rows, heads, columns // heads)
    shapes, operands = [pltpu.HBM(shape, kind)], [*lefts, *rights]
    specs = [pl.BlockSpec(memory_space=pltpu.VMEM)] * len(operands)
    if array is not None:
        shapes.append(pltpu.HBM(array.shape, array.dtype))
        operands.append(pltpu.with_memory_space_constraint(array, pltpu.VMEM))
        specs.append(pl.BlockSpec(memory_space=pl.ANY))
    return pl.pallas_call(
        functools.partial(product_kernel, len(lefts)),
        out_shape=shapes,
        in_specs=specs,
        out_specs=[pl.BlockSpec(memory_space=pl.ANY)] * len(shapes),
        scratch_shapes=[
            pltpu.VMEM((steps, rows // steps) + shape[1:], kind),
            pltpu.SemaphoreType.DMA((steps + 1,)),
        ],
        cost_estimate=pl.CostEstimate(
            flops=2 * sum(left.size for left in lefts) * columns,
            bytes_accessed=4 * rows * columns,
            transcendentals=0,
        ),
        compiler_params=pltpu.CompilerParams(vmem_limit_bytes=16 << 20),
    )(*operands)


def work(mask, inputs, fwd_positions, weight, stash, key_grad, bwd_positions):
    width, heads, head_size = weight.shape
    rows = inputs.shape[0]

    replicas = lax.axis_size("dp")
    replica = lax.axis_index("dp")
    share = width // replicas
    square = lax.axis_size("section") == 4 and mask == 2
    cut = rows // 4 if square else rows
    held = [swapped(stash[:cut], "section", mask)]
    if square:
        held.append(swapped(stash[cut:], "section", mask))

    def block_of(owner):
        start = owner * share
        return jnp.concatenate(
            [lax.dynamic_slice_in_dim(piece, start, share, 1) for piece in held]
        )

    blocks = [block_of((replica + j) % replicas) for j in range(replicas)]
    flat_weight = weight.reshape(width, heads * head_size)

    back_cos, back_sin = rope_tables(bwd_positions, head_size)
    grad_pre = rotate(
        key_grad.astype(jnp.float32), back_cos[:, None], back_sin[:, None], -1.0
    ).astype(jnp.bfloat16)
    grad_flat = grad_pre.reshape(rows, heads * head_size)
    copies = jnp.broadcast_to(grad_flat, (replicas, *grad_flat.shape))
    grads_all = exchanged(after(copies, held[0]) if square else copies)
    grads_all = [
        lax.dynamic_index_in_dim(grads_all, (replica - j) % replicas, 0, keepdims=False)
        for j in range(replicas)
    ]

    input_grad = jnp.einsum(
        "rn,dn->rd", grad_flat, flat_weight, preferred_element_type=jnp.float32
    ).astype(jnp.bfloat16)
    if square:
        half = rows // 2
        upper, lower, ahead = after((input_grad[:half], input_grad[half:], inputs), held[0])
        odd = lax.axis_index("section") % 2 == 1
        upper = swapped(upper, "section", 1)
        lower_by_2 = lax.ppermute(lower, "section", [(0, 2), (2, 0)])
        evicted = swapped(ahead, "section", mask)
        upper_by_2 = lax.ppermute(after(upper, blocks), "section", [(1, 3), (3, 1)])
        lower = swapped(jnp.where(odd, lower, after(lower_by_2, blocks)), "section", 1)
        grad_in = [(upper, upper_by_2), lower]
        blocks[-1] = after(blocks[-1], upper)
    else:
        evicted = swapped(inputs, "section", mask)
        most = rows * 3 // 4
        grad_in = [shifted(after(input_grad[:most], blocks), "section", -1)]
        rest = input_grad[most:]

    rows_all = [shifted(block, "dp", j) if j else block for j, block in enumerate(blocks)]

    if not square:
        grad_in.append(shifted(after(rest, rows_all[1]), "section", -1))

    products = jnp.dot(
        after(inputs, rows_all[1]),
        flat_weight,
        preferred_element_type=jnp.float32,
    )
    members = lax.axis_size("tensor")
    me = lax.axis_index("tensor")
    my_rows = rows // members
    summed = lax.dynamic_slice_in_dim(products, me * my_rows, my_rows, 0)
    for j in range(1, members):
        other = lax.dynamic_slice_in_dim(products, (me + j) % members * my_rows, my_rows, 0)
        summed = summed + shifted(other.astype(jnp.bfloat16), "tensor", j).astype(jnp.float32)
    my_positions = lax.dynamic_slice_in_dim(fwd_positions, me * my_rows, my_rows, 0)
    cosine, sine = rope_tables(my_positions, head_size)
    key_out = rotate(
        summed.reshape(my_rows, heads, head_size), cosine[:, None], sine[:, None], 1.0
    ).astype(jnp.bfloat16)

    lefts = [jnp.concatenate(rows_all[:-1], 0), rows_all[-1]]
    rights = [jnp.concatenate(grads_all[:-1], 0), grads_all[-1]]
    if square:
        (weight_grad,) = summed_products(lefts, rights, heads)
        grad_in, evicted = after((grad_in, evicted), weight_grad)
        key_out, grad_in, evicted = stored([key_out], grad_in, [evicted])
    else:
        weight_grad, evicted = summed_products(lefts, rights, heads, evicted)
        key_out, grad_in = finished(key_out, grad_in[1], begun(grad_in[0], rows))
    return key_out, grad_in, evicted, weight_grad


def body(fwd_input, fwd_positions, key_weight, stash, partner, key_grad, bwd_positions):
    sections = lax.axis_size("section")
    first = sections // 2
    branches = [
        lambda *blocks, mask=mask: work(mask, *blocks) for mask in range(first, sections)
    ]
    key_out, grad_in, evicted, weight_grad = lax.switch(
        partner[0] - first,
        branches,
        fwd_input[0, 0],
        fwd_positions[0, 0],
        key_weight[0],
        stash[0, 0],
        key_grad[0, 0],
        bwd_positions[0, 0],
    )
    return key_out[None, None], grad_in[None, None], evicted[None, None], weight_grad[None]


def solution(mesh):
    placed = (
        P("dp", "section", None, "tensor"),
        P("dp", "section", None),
        P("section", "tensor", None, None),
        P("dp", "section", None, "tensor"),
        P(),
        P("dp", "section", None, None, None),
        P("dp", "section", None),
    )
    return jax.shard_map(
        body,
        mesh=mesh,
        in_specs=placed,
        out_specs=(
            P("dp", "section", "tensor", None, None),
            P("dp", "section", None, "tensor"),
            P("dp", "section", None, "tensor"),
            P("section", ("tensor", "dp"), None, None),
        ),
        check_vma=False,
    )
```

```python
import functools

import jax
import jax.numpy as jnp
from jax import lax
from jax.experimental import pallas as pl
from jax.experimental.pallas import tpu as pltpu
from jax.sharding import PartitionSpec as P

THETA = 500000.0


def shifted(value, axis, distance):
    size = lax.axis_size(axis)
    return lax.ppermute(value, axis, [(i, (i + distance) % size) for i in range(size)])


def swapped(value, axis, mask):
    size = lax.axis_size(axis)
    return lax.ppermute(value, axis, [(i, i ^ mask) for i in range(size)])


def exchanged(blocks, groups=None):
    return lax.all_to_all(blocks, "dp", 0, 0, axis_index_groups=groups, tiled=True)


def after(value, earlier):
    return lax.optimization_barrier((value, earlier))[0]


def rope_tables(positions, head_size):
    half = head_size // 2
    freqs = THETA ** (-(2.0 * jnp.arange(half, dtype=jnp.float32)) / head_size)
    angles = positions.astype(jnp.float32)[..., None] * freqs
    return (jnp.cos(angles), jnp.sin(angles))


def rotate(keys, cosine, sine, sign):
    half = keys.shape[-1] // 2
    first = keys[..., :half]
    second = keys[..., half:]
    return jnp.concatenate(
        [first * cosine - sign * second * sine, second * cosine + sign * first * sine], axis=-1
    )


def store_kernel(places, *refs):
    outs = max(out for out, _, _ in places) + 1
    parts, outs, sems = refs[: -1 - outs], refs[-1 - outs : -1], refs[-1]
    parts = list(parts)
    copies = []
    for i, (out, row, choice) in enumerate(places):
        part = parts.pop(0)
        rows = outs[out].at[pl.ds(row, part.shape[0])]
        copies.append(pltpu.make_async_copy(part, rows, sems.at[i]))
        if choice:
            other = pltpu.make_async_copy(parts.pop(0), rows, sems.at[i])
            odd = lax.axis_index("section") % 2 == 1
            pl.when(odd)(other.start)
            pl.when(jnp.logical_not(odd))(copies[i].start)
        else:
            copies[i].start()
    for copy in copies:
        copy.wait()


def stored(*groups):
    places, shapes, parts = [], [], []
    for out, group in enumerate(groups):
        row = 0
        for part in group:
            choice = isinstance(part, tuple)
            parts.extend(part if choice else [part])
            places.append((out, row, choice))
            row += parts[-1].shape[0]
        shapes.append(pltpu.HBM((row,) + parts[-1].shape[1:], parts[-1].dtype))
    parts = [pltpu.with_memory_space_constraint(part, pltpu.VMEM) for part in parts]
    size = sum(part.size * part.dtype.itemsize for part in parts)
    return pl.pallas_call(
        functools.partial(store_kernel, tuple(places)),
        out_shape=shapes,
        in_specs=[pl.BlockSpec(memory_space=pl.ANY)] * len(parts),
        out_specs=[pl.BlockSpec(memory_space=pl.ANY)] * len(groups),
        scratch_shapes=[pltpu.SemaphoreType.DMA((len(places),))],
        cost_estimate=pl.CostEstimate(flops=0, bytes_accessed=2 * size, transcendentals=0),
        compiler_params=pltpu.CompilerParams(vmem_limit_bytes=1 << 20),
    )(*parts)


def finish_kernel(key_part, part, _, key_out, out, sems):
    rows = out.at[pl.ds(out.shape[0] - part.shape[0], part.shape[0])]
    copies = [
        pltpu.make_async_copy(key_part, key_out, sems.at[0]),
        pltpu.make_async_copy(part, rows, sems.at[1]),
    ]
    for copy in copies:
        copy.start()
    for copy in copies:
        copy.wait()


def finished(keys, part, into):
    parts = [pltpu.with_memory_space_constraint(x, pltpu.VMEM) for x in (keys, part)]
    size = sum(x.size * x.dtype.itemsize for x in parts)
    return pl.pallas_call(
        finish_kernel,
        out_shape=[pltpu.HBM(x.shape, x.dtype) for x in (keys, into)],
        in_specs=[pl.BlockSpec(memory_space=pl.ANY)] * 3,
        out_specs=[pl.BlockSpec(memory_space=pl.ANY)] * 2,
        scratch_shapes=[pltpu.SemaphoreType.DMA((2,))],
        input_output_aliases={2: 1},
        cost_estimate=pl.CostEstimate(flops=0, bytes_accessed=2 * size, transcendentals=0),
        compiler_params=pltpu.CompilerParams(vmem_limit_bytes=1 << 20),
    )(*parts, pltpu.with_memory_space_constraint(into, pltpu.HBM))


def begin_kernel(part, out, sem):
    copy = pltpu.make_async_copy(part, out.at[pl.ds(0, part.shape[0])], sem)
    copy.start()
    copy.wait()


def begun(part, rows):
    return pl.pallas_call(
        begin_kernel,
        out_shape=pltpu.HBM((rows,) + part.shape[1:], part.dtype),
        in_specs=[pl.BlockSpec(memory_space=pl.ANY)],
        out_specs=pl.BlockSpec(memory_space=pl.ANY),
        scratch_shapes=[pltpu.SemaphoreType.DMA],
        cost_estimate=pl.CostEstimate(
            flops=0, bytes_accessed=2 * part.size * part.dtype.itemsize, transcendentals=0
        ),
        compiler_params=pltpu.CompilerParams(vmem_limit_bytes=1 << 20),
    )(pltpu.with_memory_space_constraint(part, pltpu.VMEM))


def piece_kernel(start, array, out, sem):
    copy = pltpu.make_async_copy(array.at[pl.ds(start, out.shape[0])], out, sem)
    copy.start()
    copy.wait()


def piece(array, start, count):
    shape = (count,) + array.shape[1:]
    return pl.pallas_call(
        functools.partial(piece_kernel, start),
        out_shape=pltpu.VMEM(shape, array.dtype),
        in_specs=[pl.BlockSpec(memory_space=pl.ANY)],
        out_specs=pl.BlockSpec(memory_space=pl.ANY),
        scratch_shapes=[pltpu.SemaphoreType.DMA],
        cost_estimate=pl.CostEstimate(
            flops=0, bytes_accessed=2 * array.size // 4, transcendentals=0
        ),
        compiler_params=pltpu.CompilerParams(vmem_limit_bytes=1 << 20),
    )(pltpu.with_memory_space_constraint(array, pltpu.HBM))


def product_kernel(count, *refs):
    lefts, rights, refs = refs[:count], refs[count : 2 * count], refs[2 * count :]
    copies = []
    if len(refs) == 3:
        out, buffer, sems = refs
    else:
        array, out, array_out, buffer, sems = refs
        copies.append(pltpu.make_async_copy(array, array_out, sems.at[buffer.shape[0]]))
        copies[0].start()
    steps, step, heads, _ = buffer.shape
    for i in range(steps):
        total = sum(
            lax.dot_general(
                left[:, i * step : (i + 1) * step],
                right[...],
                (((0,), (0,)), ((), ())),
                preferred_element_type=jnp.float32,
            )
            for left, right in zip(lefts, rights)
        )
        buffer[i] = pltpu.einshape("a(bc)->abc", total, b=heads).astype(out.dtype)
        copies.append(
            pltpu.make_async_copy(buffer.at[i], out.at[pl.ds(i * step, step)], sems.at[i])
        )
        copies[-1].start()
    for copy in copies:
        copy.wait()


def summed_products(lefts, rights, heads, array=None):
    rows, columns = lefts[0].shape[1], rights[0].shape[1]
    steps = 4 if rows % 1024 == 0 else 1
    kind = lefts[0].dtype
    shape = (rows, heads, columns // heads)
    shapes, operands = [pltpu.HBM(shape, kind)], [*lefts, *rights]
    specs = [pl.BlockSpec(memory_space=pltpu.VMEM)] * len(operands)
    if array is not None:
        shapes.append(pltpu.HBM(array.shape, array.dtype))
        operands.append(pltpu.with_memory_space_constraint(array, pltpu.VMEM))
        specs.append(pl.BlockSpec(memory_space=pl.ANY))
    return pl.pallas_call(
        functools.partial(product_kernel, len(lefts)),
        out_shape=shapes,
        in_specs=specs,
        out_specs=[pl.BlockSpec(memory_space=pl.ANY)] * len(shapes),
        scratch_shapes=[
            pltpu.VMEM((steps, rows // steps) + shape[1:], kind),
            pltpu.SemaphoreType.DMA((steps + 1,)),
        ],
        cost_estimate=pl.CostEstimate(
            flops=2 * sum(left.size for left in lefts) * columns,
            bytes_accessed=4 * rows * columns,
            transcendentals=0,
        ),
        compiler_params=pltpu.CompilerParams(vmem_limit_bytes=16 << 20),
    )(*operands)


def work(mask, inputs, fwd_positions, weight, stash, key_grad, bwd_positions):
    width, heads, head_size = weight.shape
    rows = inputs.shape[0]

    replicas = lax.axis_size("dp")
    replica = lax.axis_index("dp")
    share = width // replicas
    square = lax.axis_size("section") == 4 and mask == 2
    cut = rows // 4 if square else rows
    held = [swapped(piece(stash, 0, cut) if square else stash, "section", mask)]
    if square:
        held.append(swapped(piece(stash, cut, rows - cut), "section", mask))

    def block_of(owner):
        start = owner * share
        return jnp.concatenate(
            [lax.dynamic_slice_in_dim(piece, start, share, 1) for piece in held]
        )

    blocks = [block_of((replica + j) % replicas) for j in range(replicas)]
    flat_weight = weight.reshape(width, heads * head_size)

    back_cos, back_sin = rope_tables(bwd_positions, head_size)
    grad_pre = rotate(
        key_grad.astype(jnp.float32), back_cos[:, None], back_sin[:, None], -1.0
    ).astype(jnp.bfloat16)
    grad_flat = grad_pre.reshape(rows, heads * head_size)
    copies = jnp.broadcast_to(grad_flat, (replicas, *grad_flat.shape))
    grads_all = exchanged(after(copies, held[0]) if square else copies)
    grads_all = [
        lax.dynamic_index_in_dim(grads_all, (replica - j) % replicas, 0, keepdims=False)
        for j in range(replicas)
    ]

    input_grad = jnp.einsum(
        "rn,dn->rd", grad_flat, flat_weight, preferred_element_type=jnp.float32
    ).astype(jnp.bfloat16)
    if square:
        half = rows // 2
        upper, lower, ahead = after((input_grad[:half], input_grad[half:], inputs), held[0])
        odd = lax.axis_index("section") % 2 == 1
        upper = swapped(upper, "section", 1)
        lower_by_2 = lax.ppermute(lower, "section", [(0, 2), (2, 0)])
        evicted = swapped(ahead, "section", mask)
        upper_by_2 = lax.ppermute(after(upper, blocks), "section", [(1, 3), (3, 1)])
        lower = swapped(jnp.where(odd, lower, after(lower_by_2, blocks)), "section", 1)
        grad_in = [(upper, upper_by_2), lower]
        blocks[-1] = after(blocks[-1], upper)
    else:
        evicted = swapped(inputs, "section", mask)
        most = rows * 3 // 4
        grad_in = [shifted(after(input_grad[:most], blocks), "section", -1)]
        rest = input_grad[most:]

    rows_all = [shifted(block, "dp", j) if j else block for j, block in enumerate(blocks)]

    if not square:
        grad_in.append(shifted(after(rest, rows_all[1]), "section", -1))

    products = jnp.dot(
        after(inputs, rows_all[1]),
        flat_weight,
        preferred_element_type=jnp.float32,
    )
    members = lax.axis_size("tensor")
    me = lax.axis_index("tensor")
    my_rows = rows // members
    summed = lax.dynamic_slice_in_dim(products, me * my_rows, my_rows, 0)
    for j in range(1, members):
        other = lax.dynamic_slice_in_dim(products, (me + j) % members * my_rows, my_rows, 0)
        summed = summed + shifted(other.astype(jnp.bfloat16), "tensor", j).astype(jnp.float32)
    my_positions = lax.dynamic_slice_in_dim(fwd_positions, me * my_rows, my_rows, 0)
    cosine, sine = rope_tables(my_positions, head_size)
    key_out = rotate(
        summed.reshape(my_rows, heads, head_size), cosine[:, None], sine[:, None], 1.0
    ).astype(jnp.bfloat16)

    lefts = [jnp.concatenate(rows_all[:-1], 0), rows_all[-1]]
    rights = [jnp.concatenate(grads_all[:-1], 0), grads_all[-1]]
    if square:
        (weight_grad,) = summed_products(lefts, rights, heads)
        grad_in, evicted = after((grad_in, evicted), weight_grad)
        key_out, grad_in, evicted = stored([key_out], grad_in, [evicted])
    else:
        weight_grad, evicted = summed_products(lefts, rights, heads, evicted)
        key_out, grad_in = finished(key_out, grad_in[1], begun(grad_in[0], rows))
    return key_out, grad_in, evicted, weight_grad


def body(fwd_input, fwd_positions, key_weight, stash, partner, key_grad, bwd_positions):
    sections = lax.axis_size("section")
    first = sections // 2
    branches = [
        lambda *blocks, mask=mask: work(mask, *blocks) for mask in range(first, sections)
    ]
    key_out, grad_in, evicted, weight_grad = lax.switch(
        partner[0] - first,
        branches,
        fwd_input[0, 0],
        fwd_positions[0, 0],
        key_weight[0],
        stash[0, 0],
        key_grad[0, 0],
        bwd_positions[0, 0],
    )
    return key_out[None, None], grad_in[None, None], evicted[None, None], weight_grad[None]


def solution(mesh):
    placed = (
        P("dp", "section", None, "tensor"),
        P("dp", "section", None),
        P("section", "tensor", None, None),
        P("dp", "section", None, "tensor"),
        P(),
        P("dp", "section", None, None, None),
        P("dp", "section", None),
    )
    return jax.shard_map(
        body,
        mesh=mesh,
        in_specs=placed,
        out_specs=(
            P("dp", "section", "tensor", None, None),
            P("dp", "section", None, "tensor"),
            P("dp", "section", None, "tensor"),
            P("section", ("tensor", "dp"), None, None),
        ),
        check_vma=False,
    )
```

```python
import functools

import jax
import jax.numpy as jnp
from jax import lax
from jax.experimental import pallas as pl
from jax.experimental.pallas import tpu as pltpu
from jax.sharding import PartitionSpec as P

THETA = 500000.0


def shifted(value, axis, distance):
    size = lax.axis_size(axis)
    return lax.ppermute(value, axis, [(i, (i + distance) % size) for i in range(size)])


def swapped(value, axis, mask):
    size = lax.axis_size(axis)
    return lax.ppermute(value, axis, [(i, i ^ mask) for i in range(size)])


def exchanged(blocks, groups=None):
    return lax.all_to_all(blocks, "dp", 0, 0, axis_index_groups=groups, tiled=True)


def after(value, earlier):
    return lax.optimization_barrier((value, earlier))[0]


def rope_tables(positions, head_size):
    half = head_size // 2
    freqs = THETA ** (-(2.0 * jnp.arange(half, dtype=jnp.float32)) / head_size)
    angles = positions.astype(jnp.float32)[..., None] * freqs
    return (jnp.cos(angles), jnp.sin(angles))


def rotate(keys, cosine, sine, sign):
    half = keys.shape[-1] // 2
    first = keys[..., :half]
    second = keys[..., half:]
    return jnp.concatenate(
        [first * cosine - sign * second * sine, second * cosine + sign * first * sine], axis=-1
    )


def store_kernel(places, *refs):
    outs = max(out for out, _, _ in places) + 1
    parts, outs, sems = refs[: -1 - outs], refs[-1 - outs : -1], refs[-1]
    parts = list(parts)
    copies = []
    for i, (out, row, choice) in enumerate(places):
        part = parts.pop(0)
        rows = outs[out].at[pl.ds(row, part.shape[0])]
        copies.append(pltpu.make_async_copy(part, rows, sems.at[i]))
        if choice:
            other = pltpu.make_async_copy(parts.pop(0), rows, sems.at[i])
            odd = lax.axis_index("section") % 2 == 1
            pl.when(odd)(other.start)
            pl.when(jnp.logical_not(odd))(copies[i].start)
        else:
            copies[i].start()
    for copy in copies:
        copy.wait()


def stored(*groups):
    places, shapes, parts = [], [], []
    for out, group in enumerate(groups):
        row = 0
        for part in group:
            choice = isinstance(part, tuple)
            parts.extend(part if choice else [part])
            places.append((out, row, choice))
            row += parts[-1].shape[0]
        shapes.append(pltpu.HBM((row,) + parts[-1].shape[1:], parts[-1].dtype))
    parts = [pltpu.with_memory_space_constraint(part, pltpu.VMEM) for part in parts]
    size = sum(part.size * part.dtype.itemsize for part in parts)
    return pl.pallas_call(
        functools.partial(store_kernel, tuple(places)),
        out_shape=shapes,
        in_specs=[pl.BlockSpec(memory_space=pl.ANY)] * len(parts),
        out_specs=[pl.BlockSpec(memory_space=pl.ANY)] * len(groups),
        scratch_shapes=[pltpu.SemaphoreType.DMA((len(places),))],
        cost_estimate=pl.CostEstimate(flops=0, bytes_accessed=2 * size, transcendentals=0),
        compiler_params=pltpu.CompilerParams(vmem_limit_bytes=1 << 20),
    )(*parts)


def finish_kernel(key_part, part, _, key_out, out, sems):
    rows = out.at[pl.ds(out.shape[0] - part.shape[0], part.shape[0])]
    copies = [
        pltpu.make_async_copy(key_part, key_out, sems.at[0]),
        pltpu.make_async_copy(part, rows, sems.at[1]),
    ]
    for copy in copies:
        copy.start()
    for copy in copies:
        copy.wait()


def finished(keys, part, into):
    parts = [pltpu.with_memory_space_constraint(x, pltpu.VMEM) for x in (keys, part)]
    size = sum(x.size * x.dtype.itemsize for x in parts)
    return pl.pallas_call(
        finish_kernel,
        out_shape=[pltpu.HBM(x.shape, x.dtype) for x in (keys, into)],
        in_specs=[pl.BlockSpec(memory_space=pl.ANY)] * 3,
        out_specs=[pl.BlockSpec(memory_space=pl.ANY)] * 2,
        scratch_shapes=[pltpu.SemaphoreType.DMA((2,))],
        input_output_aliases={2: 1},
        cost_estimate=pl.CostEstimate(flops=0, bytes_accessed=2 * size, transcendentals=0),
        compiler_params=pltpu.CompilerParams(vmem_limit_bytes=1 << 20),
    )(*parts, pltpu.with_memory_space_constraint(into, pltpu.HBM))


def begin_kernel(part, out, sem):
    copy = pltpu.make_async_copy(part, out.at[pl.ds(0, part.shape[0])], sem)
    copy.start()
    copy.wait()


def begun(part, rows):
    return pl.pallas_call(
        begin_kernel,
        out_shape=pltpu.HBM((rows,) + part.shape[1:], part.dtype),
        in_specs=[pl.BlockSpec(memory_space=pl.ANY)],
        out_specs=pl.BlockSpec(memory_space=pl.ANY),
        scratch_shapes=[pltpu.SemaphoreType.DMA],
        cost_estimate=pl.CostEstimate(
            flops=0, bytes_accessed=2 * part.size * part.dtype.itemsize, transcendentals=0
        ),
        compiler_params=pltpu.CompilerParams(vmem_limit_bytes=1 << 20),
    )(pltpu.with_memory_space_constraint(part, pltpu.VMEM))


def product_kernel(count, *refs):
    lefts, rights, refs = refs[:count], refs[count : 2 * count], refs[2 * count :]
    copies = []
    if len(refs) == 3:
        out, buffer, sems = refs
    else:
        array, out, array_out, buffer, sems = refs
        copies.append(pltpu.make_async_copy(array, array_out, sems.at[buffer.shape[0]]))
        copies[0].start()
    steps, step, heads, _ = buffer.shape
    for i in range(steps):
        total = sum(
            lax.dot_general(
                left[:, i * step : (i + 1) * step],
                right[...],
                (((0,), (0,)), ((), ())),
                preferred_element_type=jnp.float32,
            )
            for left, right in zip(lefts, rights)
        )
        buffer[i] = pltpu.einshape("a(bc)->abc", total, b=heads).astype(out.dtype)
        copies.append(
            pltpu.make_async_copy(buffer.at[i], out.at[pl.ds(i * step, step)], sems.at[i])
        )
        copies[-1].start()
    for copy in copies:
        copy.wait()


def summed_products(lefts, rights, heads, array=None):
    rows, columns = lefts[0].shape[1], rights[0].shape[1]
    steps = 4 if rows % 1024 == 0 else 1
    kind = lefts[0].dtype
    shape = (rows, heads, columns // heads)
    shapes, operands = [pltpu.HBM(shape, kind)], [*lefts, *rights]
    specs = [pl.BlockSpec(memory_space=pltpu.VMEM)] * len(operands)
    if array is not None:
        shapes.append(pltpu.HBM(array.shape, array.dtype))
        operands.append(pltpu.with_memory_space_constraint(array, pltpu.VMEM))
        specs.append(pl.BlockSpec(memory_space=pl.ANY))
    return pl.pallas_call(
        functools.partial(product_kernel, len(lefts)),
        out_shape=shapes,
        in_specs=specs,
        out_specs=[pl.BlockSpec(memory_space=pl.ANY)] * len(shapes),
        scratch_shapes=[
            pltpu.VMEM((steps, rows // steps) + shape[1:], kind),
            pltpu.SemaphoreType.DMA((steps + 1,)),
        ],
        cost_estimate=pl.CostEstimate(
            flops=2 * sum(left.size for left in lefts) * columns,
            bytes_accessed=4 * rows * columns,
            transcendentals=0,
        ),
        compiler_params=pltpu.CompilerParams(vmem_limit_bytes=16 << 20),
    )(*operands)


def work(mask, inputs, fwd_positions, weight, stash, key_grad, bwd_positions):
    width, heads, head_size = weight.shape
    rows = inputs.shape[0]

    replicas = lax.axis_size("dp")
    replica = lax.axis_index("dp")
    share = width // replicas
    square = lax.axis_size("section") == 4 and mask == 2
    cut = rows // 4 if square else rows
    held = [swapped(stash[:cut], "section", mask)]
    if square:
        held.append(swapped(stash[cut:], "section", mask))

    def block_of(owner):
        start = owner * share
        return jnp.concatenate(
            [lax.dynamic_slice_in_dim(piece, start, share, 1) for piece in held]
        )

    blocks = [block_of((replica + j) % replicas) for j in range(replicas)]
    flat_weight = weight.reshape(width, heads * head_size)

    back_cos, back_sin = rope_tables(bwd_positions, head_size)
    grad_pre = rotate(
        key_grad.astype(jnp.float32), back_cos[:, None], back_sin[:, None], -1.0
    ).astype(jnp.bfloat16)
    grad_flat = grad_pre.reshape(rows, heads * head_size)
    copies = jnp.broadcast_to(grad_flat, (replicas, *grad_flat.shape))
    grads_all = exchanged(after(copies, held[0]) if square else copies)
    grads_all = [
        lax.dynamic_index_in_dim(grads_all, (replica - j) % replicas, 0, keepdims=False)
        for j in range(replicas)
    ]

    input_grad = jnp.einsum(
        "rn,dn->rd", grad_flat, flat_weight, preferred_element_type=jnp.float32
    ).astype(jnp.bfloat16)
    if square:
        half = rows // 2
        upper, lower, ahead = after((input_grad[:half], input_grad[half:], inputs), held[0])
        odd = lax.axis_index("section") % 2 == 1
        upper = swapped(upper, "section", 1)
        lower_by_2 = lax.ppermute(lower, "section", [(0, 2), (2, 0)])
        evicted = swapped(ahead, "section", mask)
        upper_by_2 = lax.ppermute(after(upper, blocks), "section", [(1, 3), (3, 1)])
        lower = swapped(jnp.where(odd, lower, after(lower_by_2, blocks)), "section", 1)
        grad_in = [(upper, upper_by_2), lower]
        blocks[-1] = after(blocks[-1], upper)
    else:
        evicted = swapped(inputs, "section", mask)
        most = rows * 7 // 8
        grad_in = [shifted(after(input_grad[:most], blocks), "section", -1)]
        rest = input_grad[most:]

    rows_all = [shifted(block, "dp", j) if j else block for j, block in enumerate(blocks)]

    if not square:
        grad_in.append(shifted(after(rest, rows_all[1]), "section", -1))

    products = jnp.dot(
        after(inputs, rows_all[1]),
        flat_weight,
        preferred_element_type=jnp.float32,
    )
    members = lax.axis_size("tensor")
    me = lax.axis_index("tensor")
    my_rows = rows // members
    summed = lax.dynamic_slice_in_dim(products, me * my_rows, my_rows, 0)
    for j in range(1, members):
        other = lax.dynamic_slice_in_dim(products, (me + j) % members * my_rows, my_rows, 0)
        summed = summed + shifted(other.astype(jnp.bfloat16), "tensor", j).astype(jnp.float32)
    my_positions = lax.dynamic_slice_in_dim(fwd_positions, me * my_rows, my_rows, 0)
    cosine, sine = rope_tables(my_positions, head_size)
    key_out = rotate(
        summed.reshape(my_rows, heads, head_size), cosine[:, None], sine[:, None], 1.0
    ).astype(jnp.bfloat16)

    lefts = [jnp.concatenate(rows_all[:-1], 0), rows_all[-1]]
    rights = [jnp.concatenate(grads_all[:-1], 0), grads_all[-1]]
    if square:
        (weight_grad,) = summed_products(lefts, rights, heads)
        grad_in, evicted = after((grad_in, evicted), weight_grad)
        key_out, grad_in, evicted = stored([key_out], grad_in, [evicted])
    else:
        weight_grad, evicted = summed_products(lefts, rights, heads, evicted)
        key_out, grad_in = finished(key_out, grad_in[1], begun(grad_in[0], rows))
    return key_out, grad_in, evicted, weight_grad


def body(fwd_input, fwd_positions, key_weight, stash, partner, key_grad, bwd_positions):
    sections = lax.axis_size("section")
    first = sections // 2
    branches = [
        lambda *blocks, mask=mask: work(mask, *blocks) for mask in range(first, sections)
    ]
    key_out, grad_in, evicted, weight_grad = lax.switch(
        partner[0] - first,
        branches,
        fwd_input[0, 0],
        fwd_positions[0, 0],
        key_weight[0],
        stash[0, 0],
        key_grad[0, 0],
        bwd_positions[0, 0],
    )
    return key_out[None, None], grad_in[None, None], evicted[None, None], weight_grad[None]


def solution(mesh):
    placed = (
        P("dp", "section", None, "tensor"),
        P("dp", "section", None),
        P("section", "tensor", None, None),
        P("dp", "section", None, "tensor"),
        P(),
        P("dp", "section", None, None, None),
        P("dp", "section", None),
    )
    return jax.shard_map(
        body,
        mesh=mesh,
        in_specs=placed,
        out_specs=(
            P("dp", "section", "tensor", None, None),
            P("dp", "section", None, "tensor"),
            P("dp", "section", None, "tensor"),
            P("section", ("tensor", "dp"), None, None),
        ),
        check_vma=False,
    )
```
